512 devices in a mesh: src: 32 (over z, y_hi), tgt: 16 (over y_lo, x, core).
Axes of the slice: x: 4, y: 8 (y_hi: 4, y_lo: 2; y = y_hi * 2 + y_lo), z: 8, core: 2. Of those that a mesh axis runs over, the one named last changes fastest.
Arguments:
- source_points: float32 [3, 131072], P(None, 'src'), may hold values from -3.5 to 3.5, as said below
- target_points: float32 [3, 65536], P(None, 'tgt'), may hold values from -3.5 to 3.5, as said below
- source_weight: float32 [131072], P('src'), may hold values from 0.1 to 3
- target_weight: float32 [65536], P('tgt'), may hold values from 0.1 to 3
- target_start: float32 [65536], P('tgt'), may hold values from -1.2 to 1.2
- tile_source: int32 [32, 16, 12], P('src', 'tgt'), may hold values from 0 to 7, as said below
- tile_target: int32 [32, 16, 12], P('src', 'tgt'), may hold values from 0 to 7, as said below
- tile_count: int32 [32, 16], P('src', 'tgt'), may hold values from 8 to 12, as said below
Outputs:
- source_potential: float32 [131072], P('src')
- target_potential: float32 [65536], P('tgt')
- source_gradient: float32 [3, 131072], P(None, ('src', 'tgt'))
- target_gradient: float32 [3, 65536], P(None, 'tgt')
The draws below stay inside these ranges and needn't reach their ends.
Inputs may be any that keep to these rules, and one draw needn't show every extreme that they name: `source_points`: coordinates are cluster centres plus offsets. `target_points`: coordinates are cluster centres plus offsets. `tile_source`: within one block pair the live slots name distinct cluster pairs; the first 8 slots name every source cluster of the block once and every target cluster of the block once; slots from tile_count on hold 0. `tile_target`: as for tile_source. `tile_count`: some block pair uses all 12 slots.
All inputs are finite; a program needn't handle non-finite values.
Results may differ from the reference program's by a relative error of at most 0.0003.
Values sent between devices are 32-bit elements; how exact they have to be, the bound alone decides.
A program may use at most 64 MiB of HBM per device.

```python
import math
import jax
import jax.numpy as jnp
from jax import lax

CLUSTER = 512
CPD = 8
ITERS = 2
KMAX = 12
NS = 131072
NT = 65536
N_SRC = 32
N_TGT = 16


def tile_lists(key):
    shift_key, order_key, count_key, pick_key = jax.random.split(key, 4)
    shifts = jax.random.randint(shift_key, (N_SRC, N_TGT, 1), 0, CPD)
    base = jnp.arange(CPD, dtype=jnp.int32)[None, None, :]
    diag_src = jnp.broadcast_to(base, (N_SRC, N_TGT, CPD))
    diag_tgt = (base + shifts) % CPD
    others = CPD * (CPD - 1)

    def shuffled(one_key):
        return jax.random.permutation(one_key, others)
    order = jax.vmap(shuffled)(jax.random.split(order_key, N_SRC * N_TGT))
    order = order.reshape(N_SRC, N_TGT, others)[:, :, :KMAX - CPD].astype(jnp.int32)
    extra_src = order // (CPD - 1)
    extra_tgt = (extra_src + shifts + order % (CPD - 1) + 1) % CPD
    sources = jnp.concatenate([diag_src, extra_src], axis=2)
    targets = jnp.concatenate([diag_tgt, extra_tgt], axis=2)
    counts = jax.random.randint(count_key, (N_SRC * N_TGT,), CPD, KMAX + 1)
    full_at = jax.random.randint(pick_key, (), 0, N_SRC * N_TGT)
    counts = counts.at[full_at].set(KMAX).reshape(N_SRC, N_TGT).astype(jnp.int32)
    live = jnp.arange(KMAX, dtype=jnp.int32)[None, None, :] < counts[:, :, None]
    sources = jnp.where(live, sources, 0).astype(jnp.int32)
    targets = jnp.where(live, targets, 0).astype(jnp.int32)
    return (sources, targets, counts)


def draw_tile_source(key, part):
    lists = tile_lists(key)
    return lists[0]


def draw_tile_target(key, part):
    lists = tile_lists(key)
    return lists[1]


def draw_tile_count(key, part):
    lists = tile_lists(key)
    return lists[2]


def cloud(key, count, reach, normal_part):
    centre_key, normal_key = jax.random.split(key, 2)
    centres = jax.random.uniform(centre_key, (3, count // CLUSTER), jnp.float32, -reach, reach)
    normal_offsets = jnp.clip(jax.random.normal(normal_key, (3, count), jnp.float32), -3.0, 3.0)
    return jnp.repeat(centres, CLUSTER, axis=1) + normal_part * normal_offsets


def draw_source_points(key, part):
    key = jax.random.fold_in(key, 5)
    return cloud(key, NS, 2.0, 0.4)


def draw_target_points(key, part):
    key = jax.random.fold_in(key, 6)
    return cloud(key, NT, 2.0, 0.4)


def steps_of(stream_key, shape, cuts, smallest, top_value):
    def one(axis_at, blocks):
        heights = jax.random.uniform(jax.random.fold_in(jax.random.fold_in(stream_key, 6), axis_at), (blocks,), jnp.float32, smallest / len(cuts), top_value / len(cuts))
        return jnp.repeat(jnp.exp(heights), shape[axis_at] // blocks).reshape((-1,) + (1,) * (len(shape) - axis_at - 1))

    gain = one(*cuts[0])
    for cut in cuts[1:]:
        gain = gain * one(*cut)
    return gain


def bell_draw(stream_key, extent, scale, limit, pieces=(), kind=jnp.bfloat16):
    result = scale * jax.random.normal(stream_key, extent, jnp.float32)
    if pieces:
        result = result * steps_of(stream_key, extent, pieces, -0.22, 0.18)
    return jnp.clip(result, -limit, limit).astype(kind)


def setup_inputs(seed: int = 0) -> dict:
    key_list = jax.random.split(jax.random.key(seed), 9)
    return {
        "source_points": draw_source_points(jax.random.fold_in(key_list[8], 71), 0),
        "target_points": draw_target_points(jax.random.fold_in(key_list[8], 71), 0),
        "source_weight": jnp.clip(jnp.exp(math.log(3.0) - 3.4011974 * jax.random.uniform(key_list[2], (NS,), jnp.float32) ** steps_of(key_list[2], (NS,), ((0, 32),), -0.2, 0.2)), 0.1, 3.0),
        "target_weight": jnp.clip(jnp.exp(math.log(3.0) - 3.4011974 * jax.random.uniform(key_list[3], (NT,), jnp.float32) ** steps_of(key_list[3], (NT,), ((0, 16),), -0.2, 0.2)), 0.1, 3.0),
        "target_start": bell_draw(key_list[4], (NT,), 0.2, 1.2, ((0, 16),), jnp.float32),
        "tile_source": draw_tile_source(jax.random.fold_in(key_list[8], 71), 0),
        "tile_target": draw_tile_target(jax.random.fold_in(key_list[8], 71), 0),
        "tile_count": draw_tile_count(jax.random.fold_in(key_list[8], 71), 0),
    }


EPSILON = 0.02
FLOOR = -1.0e30


def tile_offsets(xs, ys):
    return [xs[c][:, None] - ys[c][None, :] for c in range(3)]


def tile_cost(offsets):
    return 0.5 * (offsets[0] * offsets[0] + offsets[1] * offsets[1] + offsets[2] * offsets[2])


def combine_parts(first, second):
    top = jnp.maximum(first[0], second[0])
    total = first[1] * jnp.exp(first[0] - top) + second[1] * jnp.exp(second[0] - top)
    return top, total


def reference(source_points, target_points, source_weight, target_weight, target_start, tile_source, tile_target, tile_count):
    slots = tile_source.shape[2]
    blocks_src = tile_source.shape[0]
    blocks_tgt = tile_source.shape[1]
    src_index = (jnp.arange(blocks_src, dtype=jnp.int32)[:, None, None] * CPD + tile_source).reshape(-1).astype(jnp.int32)
    tgt_index = (jnp.arange(blocks_tgt, dtype=jnp.int32)[None, :, None] * CPD + tile_target).reshape(-1).astype(jnp.int32)
    live_all = (jnp.arange(slots, dtype=jnp.int32)[None, None, :] < tile_count[:, :, None]).reshape(-1)
    log_source = jnp.log(source_weight)
    log_target = jnp.log(target_weight)
    tiles = (src_index, tgt_index, live_all)

    def tile_points(sc, tc):
        srow = (sc * CLUSTER).astype(jnp.int32)
        tcol = (tc * CLUSTER).astype(jnp.int32)
        xs = lax.dynamic_slice_in_dim(source_points, srow, CLUSTER, 1)
        ys = lax.dynamic_slice_in_dim(target_points, tcol, CLUSTER, 1)
        return srow, tcol, tile_offsets(xs, ys)

    def row_pass(target_pot):
        def step(carry, tile):
            tops, totals = carry
            srow, tcol, offs = tile_points(tile[0], tile[1])
            lb = lax.dynamic_slice_in_dim(log_target, tcol, CLUSTER)
            gs = lax.dynamic_slice_in_dim(target_pot, tcol, CLUSTER)
            scores = lb[None, :] + (gs[None, :] - tile_cost(offs)) / EPSILON
            part_top = jnp.max(scores, axis=1)
            part_total = jnp.sum(jnp.exp(scores - part_top[:, None]), axis=1)
            part_top = jnp.where(tile[2], part_top, FLOOR)
            part_total = jnp.where(tile[2], part_total, 0.0)
            old = (lax.dynamic_slice_in_dim(tops, srow, CLUSTER), lax.dynamic_slice_in_dim(totals, srow, CLUSTER))
            new = combine_parts(old, (part_top, part_total))
            tops = lax.dynamic_update_slice_in_dim(tops, new[0], srow, 0)
            totals = lax.dynamic_update_slice_in_dim(totals, new[1], srow, 0)
            return (tops, totals), None
        init = (jnp.full((NS,), FLOOR, jnp.float32), jnp.zeros((NS,), jnp.float32))
        (tops, totals), unused = lax.scan(step, init, tiles)
        return -EPSILON * (tops + jnp.log(totals))

    def col_pass(source_pot):
        def step(carry, tile):
            tops, totals = carry
            srow, tcol, offs = tile_points(tile[0], tile[1])
            la = lax.dynamic_slice_in_dim(log_source, srow, CLUSTER)
            fs = lax.dynamic_slice_in_dim(source_pot, srow, CLUSTER)
            scores = la[:, None] + (fs[:, None] - tile_cost(offs)) / EPSILON
            part_top = jnp.max(scores, axis=0)
            part_total = jnp.sum(jnp.exp(scores - part_top[None, :]), axis=0)
            part_top = jnp.where(tile[2], part_top, FLOOR)
            part_total = jnp.where(tile[2], part_total, 0.0)
            old = (lax.dynamic_slice_in_dim(tops, tcol, CLUSTER), lax.dynamic_slice_in_dim(totals, tcol, CLUSTER))
            new = combine_parts(old, (part_top, part_total))
            tops = lax.dynamic_update_slice_in_dim(tops, new[0], tcol, 0)
            totals = lax.dynamic_update_slice_in_dim(totals, new[1], tcol, 0)
            return (tops, totals), None
        init = (jnp.full((NT,), FLOOR, jnp.float32), jnp.zeros((NT,), jnp.float32))
        (tops, totals), unused = lax.scan(step, init, tiles)
        return -EPSILON * (tops + jnp.log(totals))

    target_pot = target_start
    source_pot = target_start[:0]
    for turn in range(ITERS):
        source_pot = row_pass(target_pot)
        target_pot = col_pass(source_pot)

    def grad_step(carry, tile):
        grad_src, grad_tgt = carry
        srow, tcol, offs = tile_points(tile[0], tile[1])
        la = lax.dynamic_slice_in_dim(log_source, srow, CLUSTER)
        lb = lax.dynamic_slice_in_dim(log_target, tcol, CLUSTER)
        fs = lax.dynamic_slice_in_dim(source_pot, srow, CLUSTER)
        gs = lax.dynamic_slice_in_dim(target_pot, tcol, CLUSTER)
        plan = jnp.exp(la[:, None] + lb[None, :] + (fs[:, None] + gs[None, :] - tile_cost(offs)) / EPSILON)
        plan = jnp.where(tile[2], plan, 0.0)
        src_part = jnp.stack([jnp.sum(plan * offs[c], axis=1) for c in range(3)])
        tgt_part = jnp.stack([-jnp.sum(plan * offs[c], axis=0) for c in range(3)])
        grad_src = lax.dynamic_update_slice_in_dim(grad_src, lax.dynamic_slice_in_dim(grad_src, srow, CLUSTER, 1) + src_part, srow, 1)
        grad_tgt = lax.dynamic_update_slice_in_dim(grad_tgt, lax.dynamic_slice_in_dim(grad_tgt, tcol, CLUSTER, 1) + tgt_part, tcol, 1)
        return (grad_src, grad_tgt), None

    init = (jnp.zeros((3, NS), jnp.float32), jnp.zeros((3, NT), jnp.float32))
    (grad_src, grad_tgt), unused = lax.scan(grad_step, init, tiles)
    return source_pot, target_pot, grad_src, grad_tgt
```

```python
import functools
import math

import jax
import jax.numpy as jnp
from jax import lax
from jax.experimental import pallas as pl
from jax.experimental.pallas import tpu as pltpu
from jax.sharding import PartitionSpec as P

ITERS = 2
CPD = 8
Y_HI = 4
EPSILON = 0.02
FLOOR = -1e30
R = math.sqrt(math.log2(math.e) / EPSILON)
BACK = EPSILON * math.log(2.0)
MESH = pl.DeviceIdType.MESH
F32 = jnp.float32
BF16 = jnp.bfloat16


def split3(v):
    one = v.astype(BF16).astype(F32)
    rest = v - one
    two = rest.astype(BF16).astype(F32)
    return one, two, rest - two


def logsum(parts):
    top = functools.reduce(jnp.maximum, parts)
    return top + jnp.log2(functools.reduce(jnp.add, [jnp.exp2(p - top) for p in parts]))


def kernel(n_src, n_tgt, slots, C, x_ref, y_ref, a_ref, b_ref, g_ref, ts_ref, tt_ref, tc_ref,
           f_out, g_out, sg_out, tg_out,
           xs, ys, xt, yt, cl, bias, tops, sums, ehi, elo, tx, gs,
           rbuf, ybuf, zbuf, xbar, xybuf, xzbuf, xtbuf, dsend, dbuf, ssem, rsem):
    n_z = n_src // Y_HI
    s = lax.axis_index("src")
    t = lax.axis_index("tgt")
    z = s // Y_HI
    h = lax.rem(s, Y_HI)
    tgt_peers = [(s, lax.rem(t + k, n_tgt)) for k in range(1, n_tgt)]
    y_peers = [(z * Y_HI + lax.rem(h + k, Y_HI), t) for k in range(1, Y_HI)]
    z_peers = [(lax.rem(z + k, n_z) * Y_HI + h, t) for k in range(1, n_z)]
    everyone = tgt_peers + y_peers + z_peers

    barrier = pltpu.get_barrier_semaphore()
    for peer in everyone:
        pl.semaphore_signal(barrier, inc=1, device_id=peer, device_id_type=MESH)

    def send(no, src, dst, peer):
        pltpu.make_async_remote_copy(src_ref=src, dst_ref=dst, send_sem=ssem.at[no], recv_sem=rsem.at[no],
                                     device_id=peer, device_id_type=MESH).start()

    def waiter(no, like):
        return pltpu.make_async_remote_copy(src_ref=like, dst_ref=like, send_sem=ssem.at[no], recv_sem=rsem.at[no],
                                            device_id=everyone[0], device_id_type=MESH)

    row8 = lax.broadcasted_iota(jnp.int32, (8, C), 0)
    row24 = lax.rem(lax.broadcasted_iota(jnp.int32, (24, C), 0), 8)
    for c in range(CPD):
        at = pl.ds(c * C, C)
        for ref, full, stat, norm, ones in ((x_ref, xt, xs, 3, 1.0), (y_ref, yt, ys, 4, 0.0)):
            p3 = ref[:, at] * R
            full[c, 0:3, :] = p3
            full[c, 3:6, :] = p3
            full[c, 6:8, :] = jnp.ones((2, C), F32)
            v = full[c]
            coord = row8 < 6
            one, two, three = split3(jnp.where(coord, v, 0.0))
            if norm == 3:
                a = jnp.where(row8 < 3, one, two) + jnp.where(row8 == 6, 1.0, 0.0)
                stat[c] = jnp.concatenate([a, jnp.where(row8 < 3, one, two), jnp.where(row8 < 3, one, three)], 0)
            else:
                stat[c] = jnp.concatenate([one, two, jnp.where(row8 < 3, three, one)], 0)
            cl[norm, c:c + 1, :] = 0.5 * jnp.sum(jnp.where(row8 < 3, v * v, 0.0), axis=0, keepdims=True)
        cl[0, c:c + 1, :] = a_ref[:, at]
        cl[1, c:c + 1, :] = b_ref[:, at]
        cl[2, c:c + 1, :] = g_ref[:, at]
    cl[0] = jnp.log2(cl[0])
    cl[1] = jnp.log2(cl[1])
    v = cl[2] * (1.0 / BACK) - cl[4]

    count = tc_ref[0, 0]

    def owners(ref):
        return [jnp.where(k < count, ref[0, 0, k], -1) for k in range(slots)]

    def tile_scores(summed, own, summed_index, own_index):
        lhs = jnp.concatenate([summed[summed_index], bias[...]], 0).astype(BF16)
        pick = jnp.where(row24 == summed_index, 1.0, 0.0)
        rhs = jnp.concatenate([own[own_index], pick], 0).astype(BF16)
        return lax.dot_general(lhs, rhs, (((0,), (0,)), ((), ())), preferred_element_type=F32)

    def set_bias(value):
        one, two, three = split3(value)
        bias[0:8, :] = one
        bias[8:16, :] = two
        bias[16:24, :] = three

    def one_pass(value, summed, own, summed_ref, own_ref):
        set_bias(value)

        def tile(k, carry):
            scores = tile_scores(summed, own, summed_ref[0, 0, k], own_ref[0, 0, k])
            top = jnp.max(scores, axis=0, keepdims=True)
            tops[pl.ds(k, 1), :] = top
            sums[pl.ds(k, 1), :] = jnp.sum(jnp.exp2(scores - top), axis=0, keepdims=True)
            return carry
        lax.fori_loop(0, slots, tile, 0)

    def merge(own_ref):
        own = owners(own_ref)
        masks = [row8 == own[k] for k in range(slots)]
        top = jnp.full((8, C), FLOOR, F32)
        for k in range(slots):
            top = jnp.maximum(top, jnp.where(masks[k], tops[k:k + 1, :], FLOOR))
        scales = [jnp.where(masks[k], jnp.exp2(tops[k:k + 1, :] - top), 0.0) for k in range(slots)]
        total = functools.reduce(jnp.add, [scales[k] * sums[k:k + 1, :] for k in range(slots)])
        return top + jnp.log2(total), scales, total

    def over_tgt(turn, local):
        buf = rbuf.at[turn]
        buf[t] = local
        for peer in tgt_peers:
            send(turn, buf.at[t], buf.at[t], peer)
        done = waiter(turn, buf.at[pl.ds(0, n_tgt - 1)])
        done.wait_recv()
        done.wait_send()
        return -logsum([buf[k] for k in range(n_tgt)])

    def over_y(turn, local):
        buf = ybuf.at[turn]
        buf[h] = local
        for peer in y_peers:
            send(2 + turn, buf.at[h], buf.at[h], peer)

    def over_y_done(turn):
        buf = ybuf.at[turn]
        done = waiter(2 + turn, buf.at[pl.ds(0, Y_HI - 1)])
        done.wait_recv()
        done.wait_send()
        return logsum([buf[k] for k in range(Y_HI)])

    def over_z(turn, local):
        buf = zbuf.at[turn]
        buf[z] = local
        for peer in z_peers:
            send(4 + turn, buf.at[z], buf.at[z], peer)

    def over_z_done(turn):
        buf = zbuf.at[turn]
        if n_z > 1:
            done = waiter(4 + turn, buf.at[pl.ds(0, n_z - 1)])
            done.wait_recv()
            done.wait_send()
        return logsum([buf[k] for k in range(n_z)])

    one_pass(cl[1] + v, ys, xs, tt_ref, ts_ref)
    local = merge(ts_ref)[0]
    pl.semaphore_wait(barrier, len(everyone))
    u = over_tgt(0, local)
    one_pass(cl[0] + u, xs, ys, ts_ref, tt_ref)
    over_y(0, merge(tt_ref)[0])
    over_z(0, over_y_done(0))
    v = -over_z_done(0)

    one_pass(cl[1] + v, ys, xs, tt_ref, ts_ref)
    u = over_tgt(1, merge(ts_ref)[0])

    set_bias(cl[0] + u)

    def last_tile(k, carry):
        p = ts_ref[0, 0, k]
        scores = tile_scores(xs, ys, p, tt_ref[0, 0, k])
        top = jnp.max(scores, axis=0, keepdims=True)
        tops[pl.ds(k, 1), :] = top
        e = jnp.exp2(scores - top)
        big = e.astype(BF16)
        small = (e - big.astype(F32)).astype(BF16)
        ehi[k] = big
        elo[k] = small
        lhs = xs[p].astype(BF16)
        out = jnp.dot(lhs, big, preferred_element_type=F32) + jnp.dot(lhs, small, preferred_element_type=F32)
        tx[k] = out
        sums[pl.ds(k, 1), :] = out[6:7, :]
        return carry
    lax.fori_loop(0, slots, last_tile, 0)

    local, scales, total = merge(tt_ref)
    over_y(1, local)
    per = 1.0 / total
    for c in range(3):
        acc = jnp.zeros((8, C), F32)
        for k in range(slots):
            rows = tx[k, c:c + 1, :] + tx[k, 3 + c:4 + c, :] + tx[k, 19 + c:20 + c, :]
            acc = acc + scales[k] * rows
        xbar[8 * c:8 * c + 8, :] = acc * per
    W = C // Y_HI

    def lanes(who):
        return pl.ds(pl.multiple_of(who * W, W), W)

    xybuf[h] = xbar[:, lanes(h)]
    for k in range(1, Y_HI):
        who = lax.rem(h + k, Y_HI)
        send(6, xbar.at[:, lanes(who)], xybuf.at[h], y_peers[k - 1])
    f_all = (u + cl[3]) * BACK
    for c in range(CPD):
        f_out[:, c * C:(c + 1) * C] = f_all[c:c + 1, :]
    both = over_y_done(1)
    over_z(1, both)
    done = waiter(6, xybuf.at[pl.ds(0, Y_HI - 1)])
    done.wait_recv()
    done.wait_send()

    def weighted(buf, weight_buf, n, total_block):
        acc = jnp.zeros((24, W), F32)
        for k in range(n):
            part = jnp.exp2(weight_buf[k, :, lanes(h)] - total_block)
            acc = acc + buf[k] * jnp.concatenate([part, part, part], 0)
        return acc

    xzbuf[z] = weighted(xybuf, ybuf.at[1], Y_HI, zbuf[1, z, :, lanes(h)])
    for peer in z_peers:
        send(7, xzbuf.at[z], xzbuf.at[z], peer)
    v = -over_z_done(1)

    cl[2] = v
    wlog = cl[1] + v
    bias[0:8, :] = wlog

    def grad_tile(k, carry):
        q = tt_ref[0, 0, k]
        w = jnp.exp2(bias[pl.ds(q, 1), :] + tops[pl.ds(k, 1), :])
        one, two, three = split3(yt[q] * w)
        lhs = jnp.concatenate([one, two, three], 0).astype(BF16)
        dims = (((1,), (1,)), ((), ()))
        out = (lax.dot_general(lhs, ehi[k], dims, preferred_element_type=F32)
               + lax.dot_general(lhs, elo[k], dims, preferred_element_type=F32))
        gs[k] = out[0:8, :] + out[8:16, :] + out[16:24, :]
        return carry
    lax.fori_loop(0, slots, grad_tile, 0)

    own = owners(ts_ref)
    share = CPD * C // n_tgt
    per_cluster = C // share
    for c in range(CPD):
        acc = jnp.zeros((8, C), F32)
        for k in range(slots):
            acc = acc + jnp.where(own[k] == c, gs[k], 0.0)
        diff = (xt[c] * acc[6:7, :] - acc) * (1.0 / R)
        for part in range(per_cluster):
            dsend[c * per_cluster + part] = diff[0:4, part * share:(part + 1) * share]
    dbuf[t] = dsend[t]
    for k in range(1, n_tgt):
        send(8, dsend.at[lax.rem(t + k, n_tgt)], dbuf.at[t], tgt_peers[k - 1])

    if n_z > 1:
        done = waiter(7, xzbuf.at[pl.ds(0, n_z - 1)])
        done.wait_recv()
        done.wait_send()
    xtbuf[h] = weighted(xzbuf, zbuf.at[1], n_z, -cl[2, :, lanes(h)])
    for peer in y_peers:
        send(9, xtbuf.at[h], xtbuf.at[h], peer)
    g_all = (cl[2] + cl[4]) * BACK
    for c in range(CPD):
        g_out[:, c * C:(c + 1) * C] = g_all[c:c + 1, :]

    done = waiter(8, dbuf.at[pl.ds(0, n_tgt - 1)])
    done.wait_recv()
    done.wait_send()
    grad = functools.reduce(jnp.add, [dbuf[k] for k in range(n_tgt)])
    sg_out[...] = grad[0:3, :]

    done = waiter(9, xtbuf.at[pl.ds(0, Y_HI - 1)])
    done.wait_recv()
    done.wait_send()
    for k in range(Y_HI):
        block = xtbuf[k] * (1.0 / R)
        for q in range(CPD):
            at = pl.ds(q * C + k * W, W)
            mean = jnp.concatenate([block[8 * c + q:8 * c + q + 1, :] for c in range(3)], 0)
            tg_out[:, at] = b_ref[:, at] * (y_ref[:, at] - mean)


def body(x, y, a, b, g, ts, tt, tc):
    n_src = lax.axis_size("src")
    n_tgt = lax.axis_size("tgt")
    slots = ts.shape[2]
    width = x.shape[1]
    C = width // CPD
    share = width // n_tgt
    n_z = n_src // Y_HI
    vmem = pl.BlockSpec(memory_space=pltpu.VMEM)
    smem = pl.BlockSpec(memory_space=pltpu.SMEM)
    V = pltpu.VMEM
    f, g1, sg, tg = pl.pallas_call(
        functools.partial(kernel, n_src, n_tgt, slots, C),
        out_shape=(jax.ShapeDtypeStruct((1, width), F32), jax.ShapeDtypeStruct((1, width), F32),
                   jax.ShapeDtypeStruct((3, share), F32), jax.ShapeDtypeStruct((3, width), F32)),
        in_specs=[vmem] * 5 + [smem] * 3,
        out_specs=(vmem,) * 4,
        scratch_shapes=[
            V((CPD, 24, C), F32), V((CPD, 24, C), F32), V((CPD, 8, C), F32), V((CPD, 8, C), F32),
            V((5, 8, C), F32), V((24, C), F32), V((16, C), F32), V((16, C), F32),
            V((slots, C, C), BF16), V((slots, C, C), BF16), V((slots, 24, C), F32), V((slots, 8, C), F32),
            V((ITERS, n_tgt, 8, C), F32), V((ITERS, Y_HI, 8, C), F32), V((ITERS, n_z, 8, C), F32),
            V((24, C), F32), V((Y_HI, 24, C // Y_HI), F32), V((n_z, 24, C // Y_HI), F32),
            V((Y_HI, 24, C // Y_HI), F32), V((n_tgt, 4, share), F32), V((n_tgt, 4, share), F32),
            pltpu.SemaphoreType.DMA((10,)), pltpu.SemaphoreType.DMA((10,)),
        ],
        compiler_params=pltpu.CompilerParams(collective_id=0, has_side_effects=True,
                                             vmem_limit_bytes=40 * 1024 * 1024),
        name="sinkhorn",
    )(x, y, a.reshape(1, -1), b.reshape(1, -1), g.reshape(1, -1), ts, tt, tc)
    return f.reshape(-1), g1.reshape(-1), sg, tg


def solution(mesh):
    return jax.shard_map(
        body,
        mesh=mesh,
        in_specs=(P(None, "src"), P(None, "tgt"), P("src"), P("tgt"), P("tgt"),
                  P("src", "tgt", None), P("src", "tgt", None), P("src", "tgt")),
        out_specs=(P("src"), P("tgt"), P(None, ("src", "tgt")), P(None, "tgt")),
        check_vma=False,
    )
```

```python
import functools
import math

import jax
import jax.numpy as jnp
from jax import lax
from jax.experimental import pallas as pl
from jax.experimental.pallas import tpu as pltpu
from jax.sharding import PartitionSpec as P

ITERS = 2
CPD = 8
Y_HI = 4
EPSILON = 0.02
FLOOR = -1e30
R = math.sqrt(math.log2(math.e) / EPSILON)
BACK = EPSILON * math.log(2.0)
MESH = pl.DeviceIdType.MESH
F32 = jnp.float32
BF16 = jnp.bfloat16


def split3(v):
    one = v.astype(BF16).astype(F32)
    rest = v - one
    two = rest.astype(BF16).astype(F32)
    return one, two, rest - two


def logsum(parts):
    top = functools.reduce(jnp.maximum, parts)
    return top + jnp.log2(functools.reduce(jnp.add, [jnp.exp2(p - top) for p in parts]))


def kernel(n_src, n_tgt, slots, C, *refs):
    ins, refs = refs[:8], refs[8:]
    (f_out, g_out, sg_out, tg_out), refs = refs[:4], refs[4:]
    held, refs = refs[:8], refs[8:]
    (xs, ys, xt, yt, cl, bias, tops, sums, held_scores, ehi, elo, tx, gs,
     rbuf, ybuf, zbuf, xbar, xybuf, xzbuf, xtbuf, dsend, dbuf, insem, ssem, rsem) = refs
    x_ref, y_ref, a_ref, b_ref, g_ref, ts_ref, tt_ref, tc_ref = held
    fetches = [pltpu.make_async_copy(ins[k], held[k], insem.at[k]) for k in range(8)]
    for fetch in fetches:
        fetch.start()
    n_z = n_src // Y_HI
    s = lax.axis_index("src")
    t = lax.axis_index("tgt")
    z = s // Y_HI
    h = lax.rem(s, Y_HI)
    n_lo = n_tgt // 8
    t_lo, t_x, t_core = t // 8, lax.rem(t // 2, 4), lax.rem(t, 2)
    steps = [(dy, dx, dc) for dy in range(n_lo) for dx in range(4) for dc in range(2)][1:]
    steps.sort(key=lambda d: -(d[0] + min(d[1], 4 - d[1]) + 0.1 * d[2]))
    tgt_at = [lax.rem(t_lo + dy, n_lo) * 8 + lax.rem(t_x + dx, 4) * 2 + lax.rem(t_core + dc, 2)
              for dy, dx, dc in steps]
    tgt_peers = [(s, at) for at in tgt_at]
    y_at = [lax.rem(h + k, Y_HI) for k in (2, 1, 3)]
    y_peers = [(z * Y_HI + at, t) for at in y_at]
    z_peers = [(lax.rem(z + k, n_z) * Y_HI + h, t)
               for k in sorted(range(1, n_z), key=lambda k: -min(k, n_z - k))]
    everyone = tgt_peers + y_peers + z_peers

    barrier = pltpu.get_barrier_semaphore()
    for peer in everyone:
        pl.semaphore_signal(barrier, inc=1, device_id=peer, device_id_type=MESH)

    def send(no, src, dst, peer):
        pltpu.make_async_remote_copy(src_ref=src, dst_ref=dst, send_sem=ssem.at[no], recv_sem=rsem.at[no],
                                     device_id=peer, device_id_type=MESH).start()

    def waiter(no, like):
        return pltpu.make_async_remote_copy(src_ref=like, dst_ref=like, send_sem=ssem.at[no], recv_sem=rsem.at[no],
                                            device_id=everyone[0], device_id_type=MESH)

    for fetch in fetches:
        fetch.wait()
    row8 = lax.broadcasted_iota(jnp.int32, (8, C), 0)
    row24 = lax.rem(lax.broadcasted_iota(jnp.int32, (24, C), 0), 8)
    for c in range(CPD):
        at = pl.ds(c * C, C)
        for ref, full, stat, norm, ones in ((x_ref, xt, xs, 3, 1.0), (y_ref, yt, ys, 4, 0.0)):
            p3 = ref[:, at] * R
            full[c, 0:3, :] = p3
            full[c, 3:6, :] = p3
            full[c, 6:8, :] = jnp.ones((2, C), F32)
            v = full[c]
            coord = row8 < 6
            one, two, three = split3(jnp.where(coord, v, 0.0))
            if norm == 3:
                a = jnp.where(row8 < 3, one, two) + jnp.where(row8 == 6, 1.0, 0.0)
                stat[c] = jnp.concatenate([a, jnp.where(row8 < 3, one, two), jnp.where(row8 < 3, one, three)], 0)
            else:
                stat[c] = jnp.concatenate([one, two, jnp.where(row8 < 3, three, one)], 0)
            cl[norm, c:c + 1, :] = 0.5 * jnp.sum(jnp.where(row8 < 3, v * v, 0.0), axis=0, keepdims=True)
        cl[0, c:c + 1, :] = a_ref[:, at]
        cl[1, c:c + 1, :] = b_ref[:, at]
        cl[2, c:c + 1, :] = g_ref[:, at]
    cl[0] = jnp.log2(cl[0])
    cl[1] = jnp.log2(cl[1])
    v = cl[2] * (1.0 / BACK) - cl[4]

    count = tc_ref[0, 0]

    def owners(ref):
        return [jnp.where(k < count, ref[0, 0, k], -1) for k in range(slots)]

    def tile_scores(summed, own, summed_index, own_index):
        lhs = jnp.concatenate([summed[summed_index], bias[...]], 0).astype(BF16)
        pick = jnp.where(row24 == summed_index, 1.0, 0.0)
        rhs = jnp.concatenate([own[own_index], pick], 0).astype(BF16)
        return lax.dot_general(lhs, rhs, (((0,), (0,)), ((), ())), preferred_element_type=F32)

    def set_bias(value):
        one, two, three = split3(value)
        bias[0:8, :] = one
        bias[8:16, :] = two
        bias[16:24, :] = three

    def one_pass(value, summed, own, summed_ref, own_ref):
        set_bias(value)

        def scores_of(k):
            scores = tile_scores(summed, own, summed_ref[0, 0, k], own_ref[0, 0, k])
            held_scores[...] = scores
            return jnp.max(scores, axis=0, keepdims=True)

        def tile(k, top):
            acc = jnp.exp2(held_scores[0:16, :] - top)
            for i in range(16, C, 16):
                acc = acc + jnp.exp2(held_scores[i:i + 16, :] - top)
            tops[pl.ds(k, 1), :] = top
            sums[pl.ds(k, 1), :] = jnp.sum(acc, axis=0, keepdims=True)
            return scores_of(jnp.minimum(k + 1, slots - 1))
        lax.fori_loop(0, slots, tile, scores_of(0), unroll=4)

    def merge(own_ref):
        own = owners(own_ref)
        masks = [row8 == own[k] for k in range(slots)]
        top = jnp.full((8, C), FLOOR, F32)
        for k in range(slots):
            top = jnp.maximum(top, jnp.where(masks[k], tops[k:k + 1, :], FLOOR))
        scales = [jnp.where(masks[k], jnp.exp2(tops[k:k + 1, :] - top), 0.0) for k in range(slots)]
        total = functools.reduce(jnp.add, [scales[k] * sums[k:k + 1, :] for k in range(slots)])
        return top + jnp.log2(total), scales, total

    def over_tgt(turn, local):
        buf = rbuf.at[turn]
        buf[t] = local
        for peer in tgt_peers:
            send(turn, buf.at[t], buf.at[t], peer)
        done = waiter(turn, buf.at[pl.ds(0, n_tgt - 1)])
        done.wait_recv()
        done.wait_send()
        return -logsum([buf[k] for k in range(n_tgt)])

    def over_y(turn, local):
        buf = ybuf.at[turn]
        buf[h] = local
        for peer in y_peers:
            send(2 + turn, buf.at[h], buf.at[h], peer)

    def over_y_done(turn):
        buf = ybuf.at[turn]
        done = waiter(2 + turn, buf.at[pl.ds(0, Y_HI - 1)])
        done.wait_recv()
        done.wait_send()
        return logsum([buf[k] for k in range(Y_HI)])

    def over_z(turn, local):
        buf = zbuf.at[turn]
        buf[z] = local
        for peer in z_peers:
            send(4 + turn, buf.at[z], buf.at[z], peer)

    def over_z_done(turn):
        buf = zbuf.at[turn]
        if n_z > 1:
            done = waiter(4 + turn, buf.at[pl.ds(0, n_z - 1)])
            done.wait_recv()
            done.wait_send()
        return logsum([buf[k] for k in range(n_z)])

    one_pass(cl[1] + v, ys, xs, tt_ref, ts_ref)
    local = merge(ts_ref)[0]
    pl.semaphore_wait(barrier, len(everyone))
    u = over_tgt(0, local)
    one_pass(cl[0] + u, xs, ys, ts_ref, tt_ref)
    over_y(0, merge(tt_ref)[0])
    over_z(0, over_y_done(0))
    v = -over_z_done(0)

    one_pass(cl[1] + v, ys, xs, tt_ref, ts_ref)
    u = over_tgt(1, merge(ts_ref)[0])

    one_pass(cl[0] + u, xs, ys, ts_ref, tt_ref)
    local, scales, _ = merge(tt_ref)
    over_y(1, local)

    def mean_tile(k, carry):
        p = ts_ref[0, 0, k]
        e = jnp.exp2(tile_scores(xs, ys, p, tt_ref[0, 0, k]) - tops[pl.ds(k, 1), :])
        big = e.astype(BF16)
        small = (e - big.astype(F32)).astype(BF16)
        lhs = xs[p].astype(BF16)
        tx[k] = jnp.dot(lhs, big, preferred_element_type=F32) + jnp.dot(lhs, small, preferred_element_type=F32)
        return carry

    first = max(slots - 4, 0) // 4 * 4
    lax.fori_loop(0, first, mean_tile, 0, unroll=4)
    both = over_y_done(1)
    over_z(1, both)
    lax.fori_loop(first, slots, mean_tile, 0, unroll=4)

    per = 1.0 / functools.reduce(jnp.add, [scales[k] * tx[k, 6:7, :] for k in range(slots)])
    for c in range(3):
        acc = jnp.zeros((8, C), F32)
        for k in range(slots):
            rows = tx[k, c:c + 1, :] + tx[k, 3 + c:4 + c, :] + tx[k, 19 + c:20 + c, :]
            acc = acc + scales[k] * rows
        xbar[8 * c:8 * c + 8, :] = acc * per
    W = C // Y_HI

    def lanes(who):
        return pl.ds(pl.multiple_of(who * W, W), W)

    xybuf[h] = xbar[:, lanes(h)]
    for at, peer in zip(y_at, y_peers):
        send(6, xbar.at[:, lanes(at)], xybuf.at[h], peer)

    row8_one = jnp.where(row8 < 3, 1.0, 0.0)
    blank = jnp.zeros((8, C), F32)

    def plan_tile(k, carry):
        p = ts_ref[0, 0, k]
        one, two, three = split3(-tops[pl.ds(k, 1), :])
        shift = jnp.where(row8 == 0, one, jnp.where(row8 == 1, two, jnp.where(row8 == 2, three, 0.0)))
        pick = jnp.where(row24 == p, 1.0, 0.0)
        lhs = jnp.concatenate([ys[tt_ref[0, 0, k]], pick, shift, blank], 0).astype(BF16)
        rhs = jnp.concatenate([xs[p], bias[...], row8_one, blank], 0).astype(BF16)
        e = jnp.exp2(lax.dot_general(lhs, rhs, (((0,), (0,)), ((), ())), preferred_element_type=F32))
        big = e.astype(BF16)
        ehi[k] = big
        elo[k] = (e - big.astype(F32)).astype(BF16)
        return carry
    lax.fori_loop(0, slots, plan_tile, 0, unroll=4)
    f_all = (u + cl[3]) * BACK
    for c in range(CPD):
        f_out[:, c * C:(c + 1) * C] = f_all[c:c + 1, :]
    done = waiter(6, xybuf.at[pl.ds(0, Y_HI - 1)])
    done.wait_recv()
    done.wait_send()

    def weighted(buf, weight_buf, n, total_block):
        acc = jnp.zeros((24, W), F32)
        for k in range(n):
            part = jnp.exp2(weight_buf[k, :, lanes(h)] - total_block)
            acc = acc + buf[k] * jnp.concatenate([part, part, part], 0)
        return acc

    xzbuf[z] = weighted(xybuf, ybuf.at[1], Y_HI, zbuf[1, z, :, lanes(h)])
    for peer in z_peers:
        send(7, xzbuf.at[z], xzbuf.at[z], peer)
    v = -over_z_done(1)

    cl[2] = v
    wlog = cl[1] + v
    bias[0:8, :] = wlog

    def grad_tile(k, carry):
        q = tt_ref[0, 0, k]
        w = jnp.exp2(bias[pl.ds(q, 1), :] + tops[pl.ds(k, 1), :])
        one, two, three = split3(yt[q] * w)
        lhs = jnp.concatenate([one, two, three], 0).astype(BF16)
        out = (jnp.dot(lhs, ehi[k], preferred_element_type=F32)
               + jnp.dot(lhs, elo[k], preferred_element_type=F32))
        gs[k] = out[0:8, :] + out[8:16, :] + out[16:24, :]
        return carry
    lax.fori_loop(0, slots, grad_tile, 0, unroll=4)

    own = owners(ts_ref)
    share = CPD * C // n_tgt
    per_cluster = C // share
    for c in range(CPD):
        acc = jnp.zeros((8, C), F32)
        for k in range(slots):
            acc = acc + jnp.where(own[k] == c, gs[k], 0.0)
        diff = (xt[c] * acc[6:7, :] - acc) * (1.0 / R)
        for part in range(per_cluster):
            dsend[c * per_cluster + part] = diff[0:4, part * share:(part + 1) * share]
    dbuf[t] = dsend[t]
    for at, peer in zip(tgt_at, tgt_peers):
        send(8, dsend.at[at], dbuf.at[t], peer)

    if n_z > 1:
        done = waiter(7, xzbuf.at[pl.ds(0, n_z - 1)])
        done.wait_recv()
        done.wait_send()
    xtbuf[h] = weighted(xzbuf, zbuf.at[1], n_z, -cl[2, :, lanes(h)])
    for peer in y_peers:
        send(9, xtbuf.at[h], xtbuf.at[h], peer)
    g_all = (cl[2] + cl[4]) * BACK
    for c in range(CPD):
        g_out[:, c * C:(c + 1) * C] = g_all[c:c + 1, :]

    done = waiter(8, dbuf.at[pl.ds(0, n_tgt - 1)])
    done.wait_recv()
    done.wait_send()
    grad = functools.reduce(jnp.add, [dbuf[k] for k in range(n_tgt)])
    sg_out[...] = grad[0:3, :]

    done = waiter(9, xtbuf.at[pl.ds(0, Y_HI - 1)])
    done.wait_recv()
    done.wait_send()
    for k in range(Y_HI):
        block = xtbuf[k] * (1.0 / R)
        for q in range(CPD):
            at = pl.ds(q * C + k * W, W)
            mean = jnp.concatenate([block[8 * c + q:8 * c + q + 1, :] for c in range(3)], 0)
            tg_out[:, at] = b_ref[:, at] * (y_ref[:, at] - mean)


def copy_kernel(*refs):
    n = len(refs) // 2
    sem = refs[-1]
    copies = [pltpu.make_async_copy(refs[k], refs[n + k], sem.at[k]) for k in range(n)]
    for copy in copies:
        copy.start()
    for copy in copies:
        copy.wait()


def hand_out(*arrays):
    n = len(arrays)
    return pl.pallas_call(
        copy_kernel,
        out_shape=tuple(jax.ShapeDtypeStruct(a.shape, a.dtype) for a in arrays),
        in_specs=[pl.BlockSpec(memory_space=pltpu.HBM)] * n,
        out_specs=(pl.BlockSpec(memory_space=pltpu.HBM),) * n,
        scratch_shapes=[pltpu.SemaphoreType.DMA((n,))],
        compiler_params=pltpu.CompilerParams(vmem_limit_bytes=56 * 1024 * 1024),
        name="hand_out",
    )(*arrays)


def body(x, y, a, b, g, ts, tt, tc):
    n_src = lax.axis_size("src")
    n_tgt = lax.axis_size("tgt")
    slots = ts.shape[2]
    width = x.shape[1]
    C = width // CPD
    share = width // n_tgt
    n_z = n_src // Y_HI
    vmem = pl.BlockSpec(memory_space=pltpu.VMEM)
    V = pltpu.VMEM
    f, g1, sg, tg = pl.pallas_call(
        functools.partial(kernel, n_src, n_tgt, slots, C),
        out_shape=(jax.ShapeDtypeStruct((1, width), F32), jax.ShapeDtypeStruct((1, width), F32),
                   jax.ShapeDtypeStruct((3, share), F32), jax.ShapeDtypeStruct((3, width), F32)),
        in_specs=[pl.BlockSpec(memory_space=pltpu.HBM)] * 8,
        out_specs=(vmem,) * 4,
        scratch_shapes=[
            V((3, width), F32), V((3, width), F32), V((1, width), F32), V((1, width), F32), V((1, width), F32),
            pltpu.SMEM((1, 1, slots), jnp.int32), pltpu.SMEM((1, 1, slots), jnp.int32),
            pltpu.SMEM((1, 1), jnp.int32),
            V((CPD, 24, C), F32), V((CPD, 24, C), F32), V((CPD, 8, C), F32), V((CPD, 8, C), F32),
            V((5, 8, C), F32), V((24, C), F32), V((16, C), F32), V((16, C), F32), V((C, C), F32),
            V((slots, C, C), BF16), V((slots, C, C), BF16), V((slots, 24, C), F32), V((slots, 8, C), F32),
            V((ITERS, n_tgt, 8, C), F32), V((ITERS, Y_HI, 8, C), F32), V((ITERS, n_z, 8, C), F32),
            V((24, C), F32), V((Y_HI, 24, C // Y_HI), F32), V((n_z, 24, C // Y_HI), F32),
            V((Y_HI, 24, C // Y_HI), F32), V((n_tgt, 4, share), F32), V((n_tgt, 4, share), F32),
            pltpu.SemaphoreType.DMA((8,)), pltpu.SemaphoreType.DMA((10,)), pltpu.SemaphoreType.DMA((10,)),
        ],
        compiler_params=pltpu.CompilerParams(collective_id=0, has_side_effects=True,
                                             vmem_limit_bytes=56 * 1024 * 1024),
        name="sinkhorn",
    )(x, y, a.reshape(1, -1), b.reshape(1, -1), g.reshape(1, -1), ts, tt, tc)
    f, g1, sg, tg = hand_out(f, g1, sg, tg)
    return f.reshape(-1), g1.reshape(-1), sg, tg


def solution(mesh):
    return jax.shard_map(
        body,
        mesh=mesh,
        in_specs=(P(None, "src"), P(None, "tgt"), P("src"), P("tgt"), P("tgt"),
                  P("src", "tgt", None), P("src", "tgt", None), P("src", "tgt")),
        out_specs=(P("src"), P("tgt"), P(None, ("src", "tgt")), P(None, "tgt")),
        check_vma=False,
    )
```

```python
import functools
import math

import jax
import jax.numpy as jnp
from jax import lax
from jax.experimental import pallas as pl
from jax.experimental.pallas import tpu as pltpu
from jax.sharding import PartitionSpec as P

ITERS = 2
CPD = 8
Y_HI = 4
EPSILON = 0.02
FLOOR = -1e30
R = math.sqrt(math.log2(math.e) / EPSILON)
BACK = EPSILON * math.log(2.0)
MESH = pl.DeviceIdType.MESH
F32 = jnp.float32
BF16 = jnp.bfloat16


def split3(v):
    one = v.astype(BF16).astype(F32)
    rest = v - one
    two = rest.astype(BF16).astype(F32)
    return one, two, rest - two


def logsum(parts):
    top = functools.reduce(jnp.maximum, parts)
    return top + jnp.log2(functools.reduce(jnp.add, [jnp.exp2(p - top) for p in parts]))


def kernel(n_src, n_tgt, slots, C, *refs):
    ins, refs = refs[:8], refs[8:]
    outs, refs = refs[:4], refs[4:]
    held, refs = refs[:8], refs[8:]
    (f_out, g_out, sg_out, tg_out), refs = refs[:4], refs[4:]
    (xs, ys, xt, yt, cl, bias, tops, sums, held_scores, exps, ehi, elo, tx, gs,
     rbuf, ybuf, zbuf, xbar, xybuf, xzbuf, xtbuf, dsend, dbuf, insem, outsem, ssem, rsem) = refs
    x_ref, y_ref, a_ref, b_ref, g_ref, ts_ref, tt_ref, tc_ref = held
    fetches = [pltpu.make_async_copy(ins[k], held[k], insem.at[k]) for k in range(8)]
    for fetch in fetches:
        fetch.start()
    stores = [pltpu.make_async_copy((f_out, g_out, sg_out, tg_out)[k], outs[k], outsem.at[k]) for k in range(4)]
    n_z = n_src // Y_HI
    s = lax.axis_index("src")
    t = lax.axis_index("tgt")
    z = s // Y_HI
    h = lax.rem(s, Y_HI)
    n_lo = n_tgt // 8
    t_lo, t_x, t_core = t // 8, lax.rem(t // 2, 4), lax.rem(t, 2)
    steps = [(dy, dx, dc) for dy in range(n_lo) for dx in range(4) for dc in range(2)][1:]
    steps.sort(key=lambda d: -(d[0] + min(d[1], 4 - d[1]) + 0.1 * d[2]))
    tgt_at = [lax.rem(t_lo + dy, n_lo) * 8 + lax.rem(t_x + dx, 4) * 2 + lax.rem(t_core + dc, 2)
              for dy, dx, dc in steps]
    tgt_peers = [(s, at) for at in tgt_at]
    y_at = [lax.rem(h + k, Y_HI) for k in (2, 1, 3)]
    y_peers = [(z * Y_HI + at, t) for at in y_at]
    z_peers = [(lax.rem(z + k, n_z) * Y_HI + h, t)
               for k in sorted(range(1, n_z), key=lambda k: -min(k, n_z - k))]
    everyone = tgt_peers + y_peers + z_peers

    barrier = pltpu.get_barrier_semaphore()
    for peer in everyone:
        pl.semaphore_signal(barrier, inc=1, device_id=peer, device_id_type=MESH)

    def send(no, src, dst, peer):
        pltpu.make_async_remote_copy(src_ref=src, dst_ref=dst, send_sem=ssem.at[no], recv_sem=rsem.at[no],
                                     device_id=peer, device_id_type=MESH).start()

    def waiter(no, like):
        return pltpu.make_async_remote_copy(src_ref=like, dst_ref=like, send_sem=ssem.at[no], recv_sem=rsem.at[no],
                                            device_id=everyone[0], device_id_type=MESH)

    for fetch in fetches:
        fetch.wait()
    row8 = lax.broadcasted_iota(jnp.int32, (8, C), 0)
    row24 = lax.rem(lax.broadcasted_iota(jnp.int32, (24, C), 0), 8)
    for c in range(CPD):
        at = pl.ds(c * C, C)
        for ref, full, stat, norm, ones in ((x_ref, xt, xs, 3, 1.0), (y_ref, yt, ys, 4, 0.0)):
            p3 = ref[:, at] * R
            full[c, 0:3, :] = p3
            full[c, 3:6, :] = p3
            full[c, 6:8, :] = jnp.ones((2, C), F32)
            v = full[c]
            coord = row8 < 6
            one, two, three = split3(jnp.where(coord, v, 0.0))
            if norm == 3:
                a = jnp.where(row8 < 3, one, two) + jnp.where(row8 == 6, 1.0, 0.0)
                stat[c] = jnp.concatenate([a, jnp.where(row8 < 3, one, two), jnp.where(row8 < 3, one, three)], 0)
            else:
                stat[c] = jnp.concatenate([one, two, jnp.where(row8 < 3, three, one)], 0)
            cl[norm, c:c + 1, :] = 0.5 * jnp.sum(jnp.where(row8 < 3, v * v, 0.0), axis=0, keepdims=True)
        cl[0, c:c + 1, :] = a_ref[:, at]
        cl[1, c:c + 1, :] = b_ref[:, at]
        cl[2, c:c + 1, :] = g_ref[:, at]
    cl[0] = jnp.log2(cl[0])
    cl[1] = jnp.log2(cl[1])
    v = cl[2] * (1.0 / BACK) - cl[4]

    count = tc_ref[0, 0]

    def owners(ref):
        return [jnp.where(k < count, ref[0, 0, k], -1) for k in range(slots)]

    def tile_scores(summed, own, summed_index, own_index):
        lhs = jnp.concatenate([summed[summed_index], bias[...]], 0).astype(BF16)
        pick = jnp.where(row24 == summed_index, 1.0, 0.0)
        rhs = jnp.concatenate([own[own_index], pick], 0).astype(BF16)
        return lax.dot_general(lhs, rhs, (((0,), (0,)), ((), ())), preferred_element_type=F32)

    def set_bias(value):
        one, two, three = split3(value)
        bias[0:8, :] = one
        bias[8:16, :] = two
        bias[16:24, :] = three

    def one_pass(value, summed, own, summed_ref, own_ref, keep=False):
        set_bias(value)

        def scores_of(k):
            scores = tile_scores(summed, own, summed_ref[0, 0, k], own_ref[0, 0, k])
            held_scores[...] = scores
            return jnp.max(scores, axis=0, keepdims=True)

        def tile(k, top):
            acc = None
            for i in range(0, C, 16):
                e = jnp.exp2(held_scores[i:i + 16, :] - top)
                if keep:
                    exps[k, i:i + 16, :] = e
                acc = e if acc is None else acc + e
            tops[pl.ds(k, 1), :] = top
            sums[pl.ds(k, 1), :] = jnp.sum(acc, axis=0, keepdims=True)
            return scores_of(jnp.minimum(k + 1, slots - 1))
        lax.fori_loop(0, slots, tile, scores_of(0), unroll=4)

    def merge(own_ref):
        own = owners(own_ref)
        masks = [row8 == own[k] for k in range(slots)]
        top = jnp.full((8, C), FLOOR, F32)
        for k in range(slots):
            top = jnp.maximum(top, jnp.where(masks[k], tops[k:k + 1, :], FLOOR))
        scales = [jnp.where(masks[k], jnp.exp2(tops[k:k + 1, :] - top), 0.0) for k in range(slots)]
        total = functools.reduce(jnp.add, [scales[k] * sums[k:k + 1, :] for k in range(slots)])
        return top + jnp.log2(total), scales, total

    def over_tgt(turn, local):
        buf = rbuf.at[turn]
        buf[t] = local
        for peer in tgt_peers:
            send(turn, buf.at[t], buf.at[t], peer)
        done = waiter(turn, buf.at[pl.ds(0, n_tgt - 1)])
        done.wait_recv()
        done.wait_send()
        return -logsum([buf[k] for k in range(n_tgt)])

    def over_y(turn, local):
        buf = ybuf.at[turn]
        buf[h] = local
        for peer in y_peers:
            send(2 + turn, buf.at[h], buf.at[h], peer)

    def over_y_done(turn):
        buf = ybuf.at[turn]
        done = waiter(2 + turn, buf.at[pl.ds(0, Y_HI - 1)])
        done.wait_recv()
        done.wait_send()
        return logsum([buf[k] for k in range(Y_HI)])

    def over_z(turn, local):
        buf = zbuf.at[turn]
        buf[z] = local
        for peer in z_peers:
            send(4 + turn, buf.at[z], buf.at[z], peer)

    def over_z_done(turn):
        buf = zbuf.at[turn]
        if n_z > 1:
            done = waiter(4 + turn, buf.at[pl.ds(0, n_z - 1)])
            done.wait_recv()
            done.wait_send()
        return logsum([buf[k] for k in range(n_z)])

    one_pass(cl[1] + v, ys, xs, tt_ref, ts_ref)
    local = merge(ts_ref)[0]
    pl.semaphore_wait(barrier, len(everyone))
    u = over_tgt(0, local)
    one_pass(cl[0] + u, xs, ys, ts_ref, tt_ref)
    over_y(0, merge(tt_ref)[0])
    over_z(0, over_y_done(0))
    v = -over_z_done(0)

    one_pass(cl[1] + v, ys, xs, tt_ref, ts_ref)
    u = over_tgt(1, merge(ts_ref)[0])

    one_pass(cl[0] + u, xs, ys, ts_ref, tt_ref, keep=True)
    local, scales, _ = merge(tt_ref)
    over_y(1, local)

    def mean_tile(k, carry):
        p = ts_ref[0, 0, k]
        e = exps[k]
        big = e.astype(BF16)
        small = (e - big.astype(F32)).astype(BF16)
        lhs = xs[p].astype(BF16)
        tx[k] = jnp.dot(lhs, big, preferred_element_type=F32) + jnp.dot(lhs, small, preferred_element_type=F32)
        return carry

    lax.fori_loop(0, slots, mean_tile, 0, unroll=4)

    per = 1.0 / functools.reduce(jnp.add, [scales[k] * tx[k, 6:7, :] for k in range(slots)])
    for c in range(3):
        acc = jnp.zeros((8, C), F32)
        for k in range(slots):
            rows = tx[k, c:c + 1, :] + tx[k, 3 + c:4 + c, :] + tx[k, 19 + c:20 + c, :]
            acc = acc + scales[k] * rows
        xbar[8 * c:8 * c + 8, :] = acc * per
    W = C // Y_HI

    def lanes(who):
        return pl.ds(pl.multiple_of(who * W, W), W)

    xybuf[h] = xbar[:, lanes(h)]
    for at, peer in zip(y_at, y_peers):
        send(6, xbar.at[:, lanes(at)], xybuf.at[h], peer)

    both = over_y_done(1)
    over_z(1, both)

    row8_one = jnp.where(row8 < 3, 1.0, 0.0)
    blank = jnp.zeros((8, C), F32)

    def plan_tile(k, carry):
        p = ts_ref[0, 0, k]
        one, two, three = split3(-tops[pl.ds(k, 1), :])
        shift = jnp.where(row8 == 0, one, jnp.where(row8 == 1, two, jnp.where(row8 == 2, three, 0.0)))
        pick = jnp.where(row24 == p, 1.0, 0.0)
        lhs = jnp.concatenate([ys[tt_ref[0, 0, k]], pick, shift, blank], 0).astype(BF16)
        rhs = jnp.concatenate([xs[p], bias[...], row8_one, blank], 0).astype(BF16)
        e = jnp.exp2(lax.dot_general(lhs, rhs, (((0,), (0,)), ((), ())), preferred_element_type=F32))
        big = e.astype(BF16)
        ehi[k] = big
        elo[k] = (e - big.astype(F32)).astype(BF16)
        return carry
    lax.fori_loop(0, slots, plan_tile, 0, unroll=4)
    f_all = (u + cl[3]) * BACK
    for c in range(CPD):
        f_out[:, c * C:(c + 1) * C] = f_all[c:c + 1, :]
    stores[0].start()
    done = waiter(6, xybuf.at[pl.ds(0, Y_HI - 1)])
    done.wait_recv()
    done.wait_send()

    def weighted(buf, weight_buf, n, total_block):
        acc = jnp.zeros((24, W), F32)
        for k in range(n):
            part = jnp.exp2(weight_buf[k, :, lanes(h)] - total_block)
            acc = acc + buf[k] * jnp.concatenate([part, part, part], 0)
        return acc

    xzbuf[z] = weighted(xybuf, ybuf.at[1], Y_HI, zbuf[1, z, :, lanes(h)])
    for peer in z_peers:
        send(7, xzbuf.at[z], xzbuf.at[z], peer)
    v = -over_z_done(1)

    cl[2] = v
    wlog = cl[1] + v
    bias[0:8, :] = wlog

    def grad_tile(k, carry):
        q = tt_ref[0, 0, k]
        w = jnp.exp2(bias[pl.ds(q, 1), :] + tops[pl.ds(k, 1), :])
        one, two, three = split3(yt[q] * w)
        lhs = jnp.concatenate([one, two, three], 0).astype(BF16)
        out = (jnp.dot(lhs, ehi[k], preferred_element_type=F32)
               + jnp.dot(lhs, elo[k], preferred_element_type=F32))
        gs[k] = out[0:8, :] + out[8:16, :] + out[16:24, :]
        return carry
    lax.fori_loop(0, slots, grad_tile, 0, unroll=4)

    own = owners(ts_ref)
    share = CPD * C // n_tgt
    per_cluster = C // share
    for c in range(CPD):
        acc = jnp.zeros((8, C), F32)
        for k in range(slots):
            acc = acc + jnp.where(own[k] == c, gs[k], 0.0)
        diff = (xt[c] * acc[6:7, :] - acc) * (1.0 / R)
        for part in range(per_cluster):
            dsend[c * per_cluster + part] = diff[0:4, part * share:(part + 1) * share]
    dbuf[t] = dsend[t]
    for at, peer in zip(tgt_at, tgt_peers):
        send(8, dsend.at[at], dbuf.at[t], peer)

    if n_z > 1:
        done = waiter(7, xzbuf.at[pl.ds(0, n_z - 1)])
        done.wait_recv()
        done.wait_send()
    xtbuf[h] = weighted(xzbuf, zbuf.at[1], n_z, -cl[2, :, lanes(h)])
    for peer in y_peers:
        send(9, xtbuf.at[h], xtbuf.at[h], peer)
    g_all = (cl[2] + cl[4]) * BACK
    for c in range(CPD):
        g_out[:, c * C:(c + 1) * C] = g_all[c:c + 1, :]
    stores[1].start()

    done = waiter(8, dbuf.at[pl.ds(0, n_tgt - 1)])
    done.wait_recv()
    done.wait_send()
    grad = functools.reduce(jnp.add, [dbuf[k] for k in range(n_tgt)])
    sg_out[...] = grad[0:3, :]
    stores[2].start()

    done = waiter(9, xtbuf.at[pl.ds(0, Y_HI - 1)])
    done.wait_recv()
    done.wait_send()
    for k in range(Y_HI):
        block = xtbuf[k] * (1.0 / R)
        for q in range(CPD):
            at = pl.ds(q * C + k * W, W)
            mean = jnp.concatenate([block[8 * c + q:8 * c + q + 1, :] for c in range(3)], 0)
            tg_out[:, at] = b_ref[:, at] * (y_ref[:, at] - mean)
    stores[3].start()
    for store in stores:
        store.wait()


def copy_kernel(*refs):
    n = (len(refs) - 1) // 3
    sem = refs[-1]
    loads = [pltpu.make_async_copy(refs[k], refs[2 * n + k], sem.at[k]) for k in range(n)]
    stores = [pltpu.make_async_copy(refs[2 * n + k], refs[n + k], sem.at[n + k]) for k in range(n)]
    for load in loads:
        load.start()
    for load, store in zip(loads, stores):
        load.wait()
        store.start()
    for store in stores:
        store.wait()


def hand_out(*arrays):
    n = len(arrays)
    return pl.pallas_call(
        copy_kernel,
        out_shape=tuple(jax.ShapeDtypeStruct(a.shape, a.dtype) for a in arrays),
        in_specs=[pl.BlockSpec(memory_space=pltpu.HBM)] * n,
        out_specs=(pl.BlockSpec(memory_space=pltpu.HBM),) * n,
        scratch_shapes=[pltpu.VMEM(a.shape, a.dtype) for a in arrays] + [pltpu.SemaphoreType.DMA((2 * n,))],
        compiler_params=pltpu.CompilerParams(vmem_limit_bytes=56 * 1024 * 1024),
        name="hand_out",
    )(*arrays)


def body(x, y, a, b, g, ts, tt, tc):
    n_src = lax.axis_size("src")
    n_tgt = lax.axis_size("tgt")
    slots = ts.shape[2]
    width = x.shape[1]
    C = width // CPD
    share = width // n_tgt
    n_z = n_src // Y_HI
    V = pltpu.VMEM
    f, g1, sg, tg = pl.pallas_call(
        functools.partial(kernel, n_src, n_tgt, slots, C),
        out_shape=(jax.ShapeDtypeStruct((1, width), F32), jax.ShapeDtypeStruct((1, width), F32),
                   jax.ShapeDtypeStruct((3, share), F32), jax.ShapeDtypeStruct((3, width), F32)),
        in_specs=[pl.BlockSpec(memory_space=pltpu.HBM)] * 8,
        out_specs=(pl.BlockSpec(memory_space=pltpu.HBM),) * 4,
        scratch_shapes=[
            V((3, width), F32), V((3, width), F32), V((1, width), F32), V((1, width), F32), V((1, width), F32),
            pltpu.SMEM((1, 1, slots), jnp.int32), pltpu.SMEM((1, 1, slots), jnp.int32),
            pltpu.SMEM((1, 1), jnp.int32),
            V((1, width), F32), V((1, width), F32), V((3, share), F32), V((3, width), F32),
            V((CPD, 24, C), F32), V((CPD, 24, C), F32), V((CPD, 8, C), F32), V((CPD, 8, C), F32),
            V((5, 8, C), F32), V((24, C), F32), V((16, C), F32), V((16, C), F32), V((C, C), F32),
            V((slots, C, C), F32), V((slots, C, C), BF16), V((slots, C, C), BF16), V((slots, 24, C), F32), V((slots, 8, C), F32),
            V((ITERS, n_tgt, 8, C), F32), V((ITERS, Y_HI, 8, C), F32), V((ITERS, n_z, 8, C), F32),
            V((24, C), F32), V((Y_HI, 24, C // Y_HI), F32), V((n_z, 24, C // Y_HI), F32),
            V((Y_HI, 24, C // Y_HI), F32), V((n_tgt, 4, share), F32), V((n_tgt, 4, share), F32),
            pltpu.SemaphoreType.DMA((8,)), pltpu.SemaphoreType.DMA((4,)), pltpu.SemaphoreType.DMA((10,)), pltpu.SemaphoreType.DMA((10,)),
        ],
        compiler_params=pltpu.CompilerParams(collective_id=0, has_side_effects=True,
                                             vmem_limit_bytes=56 * 1024 * 1024),
        name="sinkhorn",
    )(x, y, a.reshape(1, -1), b.reshape(1, -1), g.reshape(1, -1), ts, tt, tc)
    f, g1, sg, tg = hand_out(f, g1, sg, tg)
    return f.reshape(-1), g1.reshape(-1), sg, tg


def solution(mesh):
    return jax.shard_map(
        body,
        mesh=mesh,
        in_specs=(P(None, "src"), P(None, "tgt"), P("src"), P("tgt"), P("tgt"),
                  P("src", "tgt", None), P("src", "tgt", None), P("src", "tgt")),
        out_specs=(P("src"), P("tgt"), P(None, ("src", "tgt")), P(None, "tgt")),
        check_vma=False,
    )
```

```python
import functools
import math

import jax
import jax.numpy as jnp
from jax import lax
from jax.experimental import pallas as pl
from jax.experimental.pallas import tpu as pltpu
from jax.sharding import PartitionSpec as P

ITERS = 2
CPD = 8
Y_HI = 4
EPSILON = 0.02
FLOOR = -1e30
R = math.sqrt(math.log2(math.e) / EPSILON)
BACK = EPSILON * math.log(2.0)
MESH = pl.DeviceIdType.MESH
F32 = jnp.float32
BF16 = jnp.bfloat16


def split3(v):
    one = v.astype(BF16).astype(F32)
    rest = v - one
    two = rest.astype(BF16).astype(F32)
    return one, two, rest - two


def logsum(parts):
    top = functools.reduce(jnp.maximum, parts)
    return top + jnp.log2(functools.reduce(jnp.add, [jnp.exp2(p - top) for p in parts]))


def kernel(n_src, n_tgt, slots, C, *refs):
    ins, refs = refs[:8], refs[8:]
    outs, refs = refs[:4], refs[4:]
    held, refs = refs[:8], refs[8:]
    (f_out, g_out, sg_out, tg_out), refs = refs[:4], refs[4:]
    (xs, ys, xt, yt, cl, bias, tops, sums, held_scores, columns, row_scores, col_scores, ehi, elo, tx, gs,
     rbuf, ybuf, zbuf, xbar, xybuf, xzbuf, xtbuf, dsend, dbuf, insem, outsem, ssem, rsem) = refs
    x_ref, y_ref, a_ref, b_ref, g_ref, ts_ref, tt_ref, tc_ref = held
    fetches = [pltpu.make_async_copy(ins[k], held[k], insem.at[k]) for k in range(8)]
    for fetch in fetches:
        fetch.start()
    stores = [pltpu.make_async_copy((f_out, g_out, sg_out, tg_out)[k], outs[k], outsem.at[k]) for k in range(4)]
    n_z = n_src // Y_HI
    s = lax.axis_index("src")
    t = lax.axis_index("tgt")
    z = s // Y_HI
    h = lax.rem(s, Y_HI)
    n_lo = n_tgt // 8
    t_lo, t_x, t_core = t // 8, lax.rem(t // 2, 4), lax.rem(t, 2)
    steps = [(dy, dx, dc) for dy in range(n_lo) for dx in range(4) for dc in range(2)][1:]
    steps.sort(key=lambda d: -(d[0] + min(d[1], 4 - d[1]) + 0.1 * d[2]))
    tgt_at = [lax.rem(t_lo + dy, n_lo) * 8 + lax.rem(t_x + dx, 4) * 2 + lax.rem(t_core + dc, 2)
              for dy, dx, dc in steps]
    tgt_peers = [(s, at) for at in tgt_at]
    y_at = [lax.rem(h + k, Y_HI) for k in (2, 1, 3)]
    y_peers = [(z * Y_HI + at, t) for at in y_at]
    z_peers = [(lax.rem(z + k, n_z) * Y_HI + h, t)
               for k in sorted(range(1, n_z), key=lambda k: -min(k, n_z - k))]
    everyone = tgt_peers + y_peers + z_peers

    barrier = pltpu.get_barrier_semaphore()
    for peer in everyone:
        pl.semaphore_signal(barrier, inc=1, device_id=peer, device_id_type=MESH)

    def send(no, src, dst, peer):
        pltpu.make_async_remote_copy(src_ref=src, dst_ref=dst, send_sem=ssem.at[no], recv_sem=rsem.at[no],
                                     device_id=peer, device_id_type=MESH).start()

    def waiter(no, like):
        return pltpu.make_async_remote_copy(src_ref=like, dst_ref=like, send_sem=ssem.at[no], recv_sem=rsem.at[no],
                                            device_id=everyone[0], device_id_type=MESH)

    for fetch in fetches:
        fetch.wait()
    row8 = lax.broadcasted_iota(jnp.int32, (8, C), 0)
    row24 = lax.rem(lax.broadcasted_iota(jnp.int32, (24, C), 0), 8)
    for c in range(CPD):
        at = pl.ds(c * C, C)
        for ref, full, stat, norm, ones in ((x_ref, xt, xs, 3, 1.0), (y_ref, yt, ys, 4, 0.0)):
            p3 = ref[:, at] * R
            full[c, 0:3, :] = p3
            full[c, 3:6, :] = p3
            full[c, 6:8, :] = jnp.ones((2, C), F32)
            v = full[c]
            coord = row8 < 6
            one, two, three = split3(jnp.where(coord, v, 0.0))
            if norm == 3:
                a = jnp.where(row8 < 3, one, two) + jnp.where(row8 == 6, 1.0, 0.0)
                stat[c] = jnp.concatenate([a, jnp.where(row8 < 3, one, two), jnp.where(row8 < 3, one, three)], 0)
            else:
                stat[c] = jnp.concatenate([one, two, jnp.where(row8 < 3, three, one)], 0)
            cl[norm, c:c + 1, :] = 0.5 * jnp.sum(jnp.where(row8 < 3, v * v, 0.0), axis=0, keepdims=True)
        cl[0, c:c + 1, :] = a_ref[:, at]
        cl[1, c:c + 1, :] = b_ref[:, at]
        cl[2, c:c + 1, :] = g_ref[:, at]
    cl[0] = jnp.log2(cl[0])
    cl[1] = jnp.log2(cl[1])
    v = cl[2] * (1.0 / BACK) - cl[4]

    count = tc_ref[0, 0]

    def owners(ref):
        return [jnp.where(k < count, ref[0, 0, k], -1) for k in range(slots)]

    def tile_scores(summed, own, summed_index, own_index):
        lhs = jnp.concatenate([summed[summed_index], bias[...]], 0).astype(BF16)
        pick = jnp.where(row24 == summed_index, 1.0, 0.0)
        rhs = jnp.concatenate([own[own_index], pick], 0).astype(BF16)
        return lax.dot_general(lhs, rhs, (((0,), (0,)), ((), ())), preferred_element_type=F32)

    def set_bias(value):
        one, two, three = split3(value)
        bias[0:8, :] = one
        bias[8:16, :] = two
        bias[16:24, :] = three

    def first_pass(value):
        set_bias(value)

        def scores_of(k):
            scores = tile_scores(ys, xs, tt_ref[0, 0, k], ts_ref[0, 0, k])
            held_scores[...] = scores
            return jnp.max(scores, axis=0, keepdims=True)

        def tile(k, top):
            acc = None
            for i in range(0, C, 16):
                part = held_scores[i:i + 16, :]
                row_scores[k, i:i + 16, :] = part
                e = jnp.exp2(part - top)
                acc = e if acc is None else acc + e
            tops[pl.ds(k, 1), :] = top
            sums[pl.ds(k, 1), :] = jnp.sum(acc, axis=0, keepdims=True)
            return scores_of(jnp.minimum(k + 1, slots - 1))
        lax.fori_loop(0, slots, tile, scores_of(0), unroll=4)

    def kept_pass(value, scores, summed_ref, keep=None):
        turned = value.T
        for c in range(CPD):
            columns[c] = jnp.broadcast_to(turned[:, c:c + 1], (C, 128))

        def exps_at(k, i, top, acc):
            e = jnp.exp2(held_scores[i:i + 8, :] - top)
            if keep is not None:
                keep[k, i:i + 8, :] = e
            return e if acc is None else acc + e

        def biased_at(k, c, i, most):
            column = columns[c, i:i + 8, :]
            v = scores[k, i:i + 8, :] + jnp.concatenate([column] * (C // 128), 1)
            held_scores[i:i + 8, :] = v
            return v if most is None else jnp.maximum(most, v)

        def put(k, top, acc):
            tops[pl.ds(k, 1), :] = top
            sums[pl.ds(k, 1), :] = jnp.sum(acc, axis=0, keepdims=True)

        def tile(k, top):
            c = summed_ref[0, 0, k + 1]
            acc = most = None
            for i in range(0, C, 8):
                acc = exps_at(k, i, top, acc)
                most = biased_at(k + 1, c, i, most)
            put(k, top, acc)
            return jnp.max(most, axis=0, keepdims=True)

        c = summed_ref[0, 0, 0]
        most = None
        for i in range(0, C, 8):
            most = biased_at(0, c, i, most)
        top = lax.fori_loop(0, slots - 1, tile, jnp.max(most, axis=0, keepdims=True))
        acc = None
        for i in range(0, C, 8):
            acc = exps_at(slots - 1, i, top, acc)
        put(slots - 1, top, acc)

    def merge(own_ref):
        own = owners(own_ref)
        masks = [row8 == own[k] for k in range(slots)]
        top = jnp.full((8, C), FLOOR, F32)
        for k in range(slots):
            top = jnp.maximum(top, jnp.where(masks[k], tops[k:k + 1, :], FLOOR))
        scales = [jnp.where(masks[k], jnp.exp2(tops[k:k + 1, :] - top), 0.0) for k in range(slots)]
        total = functools.reduce(jnp.add, [scales[k] * sums[k:k + 1, :] for k in range(slots)])
        return top + jnp.log2(total), scales, total

    def over_tgt(turn, local):
        buf = rbuf.at[turn]
        buf[t] = local
        for peer in tgt_peers:
            send(turn, buf.at[t], buf.at[t], peer)

    def over_tgt_done(turn):
        buf = rbuf.at[turn]
        done = waiter(turn, buf.at[pl.ds(0, n_tgt - 1)])
        done.wait_recv()
        done.wait_send()
        return -logsum([buf[k] for k in range(n_tgt)])

    def over_y(turn, local):
        buf = ybuf.at[turn]
        buf[h] = local
        for peer in y_peers:
            send(2 + turn, buf.at[h], buf.at[h], peer)

    def over_y_done(turn):
        buf = ybuf.at[turn]
        done = waiter(2 + turn, buf.at[pl.ds(0, Y_HI - 1)])
        done.wait_recv()
        done.wait_send()
        return logsum([buf[k] for k in range(Y_HI)])

    def over_z(turn, local):
        buf = zbuf.at[turn]
        buf[z] = local
        for peer in z_peers:
            send(4 + turn, buf.at[z], buf.at[z], peer)

    def over_z_done(turn):
        buf = zbuf.at[turn]
        if n_z > 1:
            done = waiter(4 + turn, buf.at[pl.ds(0, n_z - 1)])
            done.wait_recv()
            done.wait_send()
        return logsum([buf[k] for k in range(n_z)])

    first_pass(cl[1] + v)
    start = v
    local = merge(ts_ref)[0]
    pl.semaphore_wait(barrier, len(everyone))
    over_tgt(0, local)

    def score_tile(k, carry):
        col_scores[k] = lax.dot_general(xs[ts_ref[0, 0, k]].astype(BF16), ys[tt_ref[0, 0, k]].astype(BF16),
                                        (((0,), (0,)), ((), ())), preferred_element_type=F32)
        return carry
    lax.fori_loop(0, slots, score_tile, 0, unroll=4)
    u = over_tgt_done(0)
    kept_pass(cl[0] + u, col_scores, ts_ref)
    over_y(0, merge(tt_ref)[0])
    over_z(0, over_y_done(0))
    v = -over_z_done(0)

    kept_pass(v - start, row_scores, tt_ref)
    over_tgt(1, merge(ts_ref)[0])
    u = over_tgt_done(1)
    exps = row_scores
    kept_pass(cl[0] + u, col_scores, ts_ref, keep=exps)
    local, scales, _ = merge(tt_ref)
    over_y(1, local)

    def mean_tile(k, carry):
        p = ts_ref[0, 0, k]
        e = exps[k]
        big = e.astype(BF16)
        small = (e - big.astype(F32)).astype(BF16)
        lhs = xs[p].astype(BF16)
        tx[k] = jnp.dot(lhs, big, preferred_element_type=F32) + jnp.dot(lhs, small, preferred_element_type=F32)
        return carry

    lax.fori_loop(0, slots, mean_tile, 0, unroll=4)

    per = 1.0 / functools.reduce(jnp.add, [scales[k] * tx[k, 6:7, :] for k in range(slots)])
    for c in range(3):
        acc = jnp.zeros((8, C), F32)
        for k in range(slots):
            rows = tx[k, c:c + 1, :] + tx[k, 3 + c:4 + c, :] + tx[k, 19 + c:20 + c, :]
            acc = acc + scales[k] * rows
        xbar[8 * c:8 * c + 8, :] = acc * per
    W = C // Y_HI

    def lanes(who):
        return pl.ds(pl.multiple_of(who * W, W), W)

    xybuf[h] = xbar[:, lanes(h)]
    for at, peer in zip(y_at, y_peers):
        send(6, xbar.at[:, lanes(at)], xybuf.at[h], peer)

    both = over_y_done(1)
    over_z(1, both)

    set_bias(cl[0] + u)
    row8_one = jnp.where(row8 < 3, 1.0, 0.0)
    blank = jnp.zeros((8, C), F32)

    def plan_tile(k, carry):
        p = ts_ref[0, 0, k]
        one, two, three = split3(-tops[pl.ds(k, 1), :])
        shift = jnp.where(row8 == 0, one, jnp.where(row8 == 1, two, jnp.where(row8 == 2, three, 0.0)))
        pick = jnp.where(row24 == p, 1.0, 0.0)
        lhs = jnp.concatenate([ys[tt_ref[0, 0, k]], pick, shift, blank], 0).astype(BF16)
        rhs = jnp.concatenate([xs[p], bias[...], row8_one, blank], 0).astype(BF16)
        e = jnp.exp2(lax.dot_general(lhs, rhs, (((0,), (0,)), ((), ())), preferred_element_type=F32))
        big = e.astype(BF16)
        ehi[k] = big
        elo[k] = (e - big.astype(F32)).astype(BF16)
        return carry
    lax.fori_loop(0, slots, plan_tile, 0, unroll=4)
    f_all = (u + cl[3]) * BACK
    for c in range(CPD):
        f_out[:, c * C:(c + 1) * C] = f_all[c:c + 1, :]
    stores[0].start()
    done = waiter(6, xybuf.at[pl.ds(0, Y_HI - 1)])
    done.wait_recv()
    done.wait_send()

    def weighted(buf, weight_buf, n, total_block):
        acc = jnp.zeros((24, W), F32)
        for k in range(n):
            part = jnp.exp2(weight_buf[k, :, lanes(h)] - total_block)
            acc = acc + buf[k] * jnp.concatenate([part, part, part], 0)
        return acc

    xzbuf[z] = weighted(xybuf, ybuf.at[1], Y_HI, zbuf[1, z, :, lanes(h)])
    for peer in z_peers:
        send(7, xzbuf.at[z], xzbuf.at[z], peer)
    v = -over_z_done(1)

    cl[2] = v
    wlog = cl[1] + v
    bias[0:8, :] = wlog

    def grad_tile(k, carry):
        q = tt_ref[0, 0, k]
        w = jnp.exp2(bias[pl.ds(q, 1), :] + tops[pl.ds(k, 1), :])
        one, two, three = split3(yt[q] * w)
        lhs = jnp.concatenate([one, two, three], 0).astype(BF16)
        out = (jnp.dot(lhs, ehi[k], preferred_element_type=F32)
               + jnp.dot(lhs, elo[k], preferred_element_type=F32))
        gs[k] = out[0:8, :] + out[8:16, :] + out[16:24, :]
        return carry
    lax.fori_loop(0, slots, grad_tile, 0, unroll=4)

    own = owners(ts_ref)
    share = CPD * C // n_tgt
    per_cluster = C // share
    for c in range(CPD):
        acc = jnp.zeros((8, C), F32)
        for k in range(slots):
            acc = acc + jnp.where(own[k] == c, gs[k], 0.0)
        diff = (xt[c] * acc[6:7, :] - acc) * (1.0 / R)
        for part in range(per_cluster):
            dsend[c * per_cluster + part] = diff[0:4, part * share:(part + 1) * share]
    dbuf[t] = dsend[t]
    for at, peer in zip(tgt_at, tgt_peers):
        send(8, dsend.at[at], dbuf.at[t], peer)

    if n_z > 1:
        done = waiter(7, xzbuf.at[pl.ds(0, n_z - 1)])
        done.wait_recv()
        done.wait_send()
    xtbuf[h] = weighted(xzbuf, zbuf.at[1], n_z, -cl[2, :, lanes(h)])
    for peer in y_peers:
        send(9, xtbuf.at[h], xtbuf.at[h], peer)
    g_all = (cl[2] + cl[4]) * BACK
    for c in range(CPD):
        g_out[:, c * C:(c + 1) * C] = g_all[c:c + 1, :]
    stores[1].start()

    done = waiter(8, dbuf.at[pl.ds(0, n_tgt - 1)])
    done.wait_recv()
    done.wait_send()
    grad = functools.reduce(jnp.add, [dbuf[k] for k in range(n_tgt)])
    sg_out[...] = grad[0:3, :]
    stores[2].start()

    done = waiter(9, xtbuf.at[pl.ds(0, Y_HI - 1)])
    done.wait_recv()
    done.wait_send()
    for k in range(Y_HI):
        block = xtbuf[k] * (1.0 / R)
        for q in range(CPD):
            at = pl.ds(q * C + k * W, W)
            mean = jnp.concatenate([block[8 * c + q:8 * c + q + 1, :] for c in range(3)], 0)
            tg_out[:, at] = b_ref[:, at] * (y_ref[:, at] - mean)
    stores[3].start()
    for store in stores:
        store.wait()


def copy_kernel(*refs):
    n = (len(refs) - 1) // 3
    sem = refs[-1]
    loads = [pltpu.make_async_copy(refs[k], refs[2 * n + k], sem.at[k]) for k in range(n)]
    stores = [pltpu.make_async_copy(refs[2 * n + k], refs[n + k], sem.at[n + k]) for k in range(n)]
    for load in loads:
        load.start()
    for load, store in zip(loads, stores):
        load.wait()
        store.start()
    for store in stores:
        store.wait()


def hand_out(*arrays):
    n = len(arrays)
    return pl.pallas_call(
        copy_kernel,
        out_shape=tuple(jax.ShapeDtypeStruct(a.shape, a.dtype) for a in arrays),
        in_specs=[pl.BlockSpec(memory_space=pltpu.HBM)] * n,
        out_specs=(pl.BlockSpec(memory_space=pltpu.HBM),) * n,
        scratch_shapes=[pltpu.VMEM(a.shape, a.dtype) for a in arrays] + [pltpu.SemaphoreType.DMA((2 * n,))],
        compiler_params=pltpu.CompilerParams(vmem_limit_bytes=56 * 1024 * 1024),
        name="hand_out",
    )(*arrays)


def body(x, y, a, b, g, ts, tt, tc):
    n_src = lax.axis_size("src")
    n_tgt = lax.axis_size("tgt")
    slots = ts.shape[2]
    width = x.shape[1]
    C = width // CPD
    share = width // n_tgt
    n_z = n_src // Y_HI
    V = pltpu.VMEM
    f, g1, sg, tg = pl.pallas_call(
        functools.partial(kernel, n_src, n_tgt, slots, C),
        out_shape=(jax.ShapeDtypeStruct((1, width), F32), jax.ShapeDtypeStruct((1, width), F32),
                   jax.ShapeDtypeStruct((3, share), F32), jax.ShapeDtypeStruct((3, width), F32)),
        in_specs=[pl.BlockSpec(memory_space=pltpu.HBM)] * 8,
        out_specs=(pl.BlockSpec(memory_space=pltpu.HBM),) * 4,
        scratch_shapes=[
            V((3, width), F32), V((3, width), F32), V((1, width), F32), V((1, width), F32), V((1, width), F32),
            pltpu.SMEM((1, 1, slots), jnp.int32), pltpu.SMEM((1, 1, slots), jnp.int32),
            pltpu.SMEM((1, 1), jnp.int32),
            V((1, width), F32), V((1, width), F32), V((3, share), F32), V((3, width), F32),
            V((CPD, 24, C), F32), V((CPD, 24, C), F32), V((CPD, 8, C), F32), V((CPD, 8, C), F32),
            V((5, 8, C), F32), V((24, C), F32), V((16, C), F32), V((16, C), F32), V((C, C), F32), V((CPD, C, 128), F32), V((slots, C, C), F32),
            V((slots, C, C), F32), V((slots, C, C), BF16), V((slots, C, C), BF16), V((slots, 24, C), F32), V((slots, 8, C), F32),
            V((ITERS, n_tgt, 8, C), F32), V((ITERS, Y_HI, 8, C), F32), V((ITERS, n_z, 8, C), F32),
            V((24, C), F32), V((Y_HI, 24, C // Y_HI), F32), V((n_z, 24, C // Y_HI), F32),
            V((Y_HI, 24, C // Y_HI), F32), V((n_tgt, 4, share), F32), V((n_tgt, 4, share), F32),
            pltpu.SemaphoreType.DMA((8,)), pltpu.SemaphoreType.DMA((4,)), pltpu.SemaphoreType.DMA((10,)), pltpu.SemaphoreType.DMA((10,)),
        ],
        compiler_params=pltpu.CompilerParams(collective_id=0, has_side_effects=True,
                                             vmem_limit_bytes=56 * 1024 * 1024),
        name="sinkhorn",
    )(x, y, a.reshape(1, -1), b.reshape(1, -1), g.reshape(1, -1), ts, tt, tc)
    f, g1, sg, tg = hand_out(f, g1, sg, tg)
    return f.reshape(-1), g1.reshape(-1), sg, tg


def solution(mesh):
    return jax.shard_map(
        body,
        mesh=mesh,
        in_specs=(P(None, "src"), P(None, "tgt"), P("src"), P("tgt"), P("tgt"),
                  P("src", "tgt", None), P("src", "tgt", None), P("src", "tgt")),
        out_specs=(P("src"), P("tgt"), P(None, ("src", "tgt")), P(None, "tgt")),
        check_vma=False,
    )
```

```python
import functools
import math

import jax
import jax.numpy as jnp
from jax import lax
from jax.experimental import pallas as pl
from jax.experimental.pallas import tpu as pltpu
from jax.sharding import PartitionSpec as P

ITERS = 2
CPD = 8
Y_HI = 4
EPSILON = 0.02
FLOOR = -1e30
R = math.sqrt(math.log2(math.e) / EPSILON)
BACK = EPSILON * math.log(2.0)
MESH = pl.DeviceIdType.MESH
F32 = jnp.float32
BF16 = jnp.bfloat16


def split3(v):
    one = v.astype(BF16).astype(F32)
    rest = v - one
    two = rest.astype(BF16).astype(F32)
    return one, two, rest - two


def logsum(parts):
    top = functools.reduce(jnp.maximum, parts)
    return top + jnp.log2(functools.reduce(jnp.add, [jnp.exp2(p - top) for p in parts]))


def kernel(n_src, n_tgt, slots, C, *refs):
    ins, refs = refs[:8], refs[8:]
    outs, refs = refs[:4], refs[4:]
    held, refs = refs[:8], refs[8:]
    (f_out, g_out, sg_out, tg_out), refs = refs[:4], refs[4:]
    (xs, ys, xt, yt, cl, bias, tops, sums, held_scores, columns, row_scores, col_scores, ehi, elo, tx, gs,
     rbuf, ybuf, zbuf, xbar, xybuf, xzbuf, xtbuf, dsend, dbuf, insem, outsem, ssem, rsem) = refs
    x_ref, y_ref, a_ref, b_ref, g_ref, ts_ref, tt_ref, tc_ref = held
    fetches = [pltpu.make_async_copy(ins[k], held[k], insem.at[k]) for k in range(8)]
    for fetch in fetches:
        fetch.start()
    stores = [pltpu.make_async_copy((f_out, g_out, sg_out, tg_out)[k], outs[k], outsem.at[k]) for k in range(4)]
    n_z = n_src // Y_HI
    s = lax.axis_index("src")
    t = lax.axis_index("tgt")
    z = s // Y_HI
    h = lax.rem(s, Y_HI)
    n_lo = n_tgt // 8
    t_lo, t_x, t_core = t // 8, lax.rem(t // 2, 4), lax.rem(t, 2)
    steps = [(dy, dx, dc) for dy in range(n_lo) for dx in range(4) for dc in range(2)][1:]
    steps.sort(key=lambda d: -(d[0] + min(d[1], 4 - d[1]) + 0.1 * d[2]))
    tgt_at = [lax.rem(t_lo + dy, n_lo) * 8 + lax.rem(t_x + dx, 4) * 2 + lax.rem(t_core + dc, 2)
              for dy, dx, dc in steps]
    tgt_peers = [(s, at) for at in tgt_at]
    y_at = [lax.rem(h + k, Y_HI) for k in (2, 1, 3)]
    y_peers = [(z * Y_HI + at, t) for at in y_at]
    z_peers = [(lax.rem(z + k, n_z) * Y_HI + h, t)
               for k in sorted(range(1, n_z), key=lambda k: -min(k, n_z - k))]
    everyone = tgt_peers + y_peers + z_peers

    barrier = pltpu.get_barrier_semaphore()
    for peer in everyone:
        pl.semaphore_signal(barrier, inc=1, device_id=peer, device_id_type=MESH)

    def send(no, src, dst, peer):
        pltpu.make_async_remote_copy(src_ref=src, dst_ref=dst, send_sem=ssem.at[no], recv_sem=rsem.at[no],
                                     device_id=peer, device_id_type=MESH).start()

    def waiter(no, like):
        return pltpu.make_async_remote_copy(src_ref=like, dst_ref=like, send_sem=ssem.at[no], recv_sem=rsem.at[no],
                                            device_id=everyone[0], device_id_type=MESH)

    for fetch in fetches:
        fetch.wait()
    row8 = lax.broadcasted_iota(jnp.int32, (8, C), 0)
    row24 = lax.rem(lax.broadcasted_iota(jnp.int32, (24, C), 0), 8)
    for c in range(CPD):
        at = pl.ds(c * C, C)
        for ref, full, stat, norm, ones in ((x_ref, xt, xs, 3, 1.0), (y_ref, yt, ys, 4, 0.0)):
            p3 = ref[:, at] * R
            full[c, 0:3, :] = p3
            full[c, 3:6, :] = p3
            full[c, 6:8, :] = jnp.ones((2, C), F32)
            v = full[c]
            coord = row8 < 6
            one, two, three = split3(jnp.where(coord, v, 0.0))
            if norm == 3:
                a = jnp.where(row8 < 3, one, two) + jnp.where(row8 == 6, 1.0, 0.0)
                stat[c] = jnp.concatenate([a, jnp.where(row8 < 3, one, two), jnp.where(row8 < 3, one, three)], 0)
            else:
                stat[c] = jnp.concatenate([one, two, jnp.where(row8 < 3, three, one)], 0)
            cl[norm, c:c + 1, :] = 0.5 * jnp.sum(jnp.where(row8 < 3, v * v, 0.0), axis=0, keepdims=True)
        cl[0, c:c + 1, :] = a_ref[:, at]
        cl[1, c:c + 1, :] = b_ref[:, at]
        cl[2, c:c + 1, :] = g_ref[:, at]
    cl[0] = jnp.log2(cl[0])
    cl[1] = jnp.log2(cl[1])
    v = cl[2] * (1.0 / BACK) - cl[4]

    count = tc_ref[0, 0]

    def owners(ref):
        return [jnp.where(k < count, ref[0, 0, k], -1) for k in range(slots)]

    def tile_scores(summed, own, summed_index, own_index):
        lhs = jnp.concatenate([summed[summed_index], bias[...]], 0).astype(BF16)
        pick = jnp.where(row24 == summed_index, 1.0, 0.0)
        rhs = jnp.concatenate([own[own_index], pick], 0).astype(BF16)
        return lax.dot_general(lhs, rhs, (((0,), (0,)), ((), ())), preferred_element_type=F32)

    def set_bias(value):
        one, two, three = split3(value)
        bias[0:8, :] = one
        bias[8:16, :] = two
        bias[16:24, :] = three

    def first_pass(value):
        set_bias(value)

        def scores_of(k):
            scores = tile_scores(ys, xs, tt_ref[0, 0, k], ts_ref[0, 0, k])
            held_scores[...] = scores
            return jnp.max(scores, axis=0, keepdims=True)

        def tile(k, top):
            acc = None
            for i in range(0, C, 16):
                part = held_scores[i:i + 16, :]
                row_scores[k, i:i + 16, :] = part
                e = jnp.exp2(part - top)
                acc = e if acc is None else acc + e
            tops[pl.ds(k, 1), :] = top
            sums[pl.ds(k, 1), :] = jnp.sum(acc, axis=0, keepdims=True)
            return scores_of(jnp.minimum(k + 1, slots - 1))
        lax.fori_loop(0, slots, tile, scores_of(0), unroll=4)

    def kept_pass(value, scores, summed_ref, keep=None):
        bias[0:8, :] = value

        def turn(k):
            row = bias[pl.ds(summed_ref[0, 0, k], 1), :]
            columns[...] = jnp.broadcast_to(row, (128, C)).T

        def exps_at(k, i, top, acc):
            e = jnp.exp2(held_scores[i:i + 8, :] - top)
            if keep is not None:
                keep[k, i:i + 8, :] = e
            return e if acc is None else acc + e

        def biased_at(k, i, most):
            column = columns[i:i + 8, :]
            v = scores[k, i:i + 8, :] + jnp.concatenate([column] * (C // 128), 1)
            held_scores[i:i + 8, :] = v
            return v if most is None else jnp.maximum(most, v)

        def put(k, top, acc):
            tops[pl.ds(k, 1), :] = top
            sums[pl.ds(k, 1), :] = jnp.sum(acc, axis=0, keepdims=True)

        def tile(k, top):
            acc = most = None
            for i in range(0, C, 8):
                acc = exps_at(k, i, top, acc)
                most = biased_at(k + 1, i, most)
            turn(jnp.minimum(k + 2, slots - 1))
            put(k, top, acc)
            return jnp.max(most, axis=0, keepdims=True)

        turn(0)
        most = None
        for i in range(0, C, 8):
            most = biased_at(0, i, most)
        turn(1)
        top = lax.fori_loop(0, slots - 1, tile, jnp.max(most, axis=0, keepdims=True))
        acc = None
        for i in range(0, C, 8):
            acc = exps_at(slots - 1, i, top, acc)
        put(slots - 1, top, acc)

    def merge(own_ref):
        own = owners(own_ref)
        masks = [row8 == own[k] for k in range(slots)]
        top = jnp.full((8, C), FLOOR, F32)
        for k in range(slots):
            top = jnp.maximum(top, jnp.where(masks[k], tops[k:k + 1, :], FLOOR))
        scales = [jnp.where(masks[k], jnp.exp2(tops[k:k + 1, :] - top), 0.0) for k in range(slots)]
        total = functools.reduce(jnp.add, [scales[k] * sums[k:k + 1, :] for k in range(slots)])
        return top + jnp.log2(total), scales, total

    def over_tgt(turn, local):
        buf = rbuf.at[turn]
        buf[t] = local
        for peer in tgt_peers:
            send(turn, buf.at[t], buf.at[t], peer)

    def over_tgt_done(turn):
        buf = rbuf.at[turn]
        done = waiter(turn, buf.at[pl.ds(0, n_tgt - 1)])
        done.wait_recv()
        done.wait_send()
        return -logsum([buf[k] for k in range(n_tgt)])

    def over_y(turn, local):
        buf = ybuf.at[turn]
        buf[h] = local
        for peer in y_peers:
            send(2 + turn, buf.at[h], buf.at[h], peer)

    def over_y_done(turn):
        buf = ybuf.at[turn]
        done = waiter(2 + turn, buf.at[pl.ds(0, Y_HI - 1)])
        done.wait_recv()
        done.wait_send()
        return logsum([buf[k] for k in range(Y_HI)])

    def over_z(turn, local):
        buf = zbuf.at[turn]
        buf[z] = local
        for peer in z_peers:
            send(4 + turn, buf.at[z], buf.at[z], peer)

    def over_z_done(turn):
        buf = zbuf.at[turn]
        if n_z > 1:
            done = waiter(4 + turn, buf.at[pl.ds(0, n_z - 1)])
            done.wait_recv()
            done.wait_send()
        return logsum([buf[k] for k in range(n_z)])

    first_pass(cl[1] + v)
    start = v
    local = merge(ts_ref)[0]
    pl.semaphore_wait(barrier, len(everyone))
    over_tgt(0, local)

    def score_tile(k, carry):
        col_scores[k] = lax.dot_general(xs[ts_ref[0, 0, k]].astype(BF16), ys[tt_ref[0, 0, k]].astype(BF16),
                                        (((0,), (0,)), ((), ())), preferred_element_type=F32)
        return carry
    lax.fori_loop(0, slots, score_tile, 0, unroll=4)
    u = over_tgt_done(0)
    kept_pass(cl[0] + u, col_scores, ts_ref)
    over_y(0, merge(tt_ref)[0])
    over_z(0, over_y_done(0))
    v = -over_z_done(0)

    kept_pass(v - start, row_scores, tt_ref)
    over_tgt(1, merge(ts_ref)[0])
    u = over_tgt_done(1)
    exps = row_scores
    kept_pass(cl[0] + u, col_scores, ts_ref, keep=exps)
    local, scales, _ = merge(tt_ref)
    over_y(1, local)

    def mean_tile(k, carry):
        p = ts_ref[0, 0, k]
        e = exps[k]
        big = e.astype(BF16)
        small = (e - big.astype(F32)).astype(BF16)
        lhs = xs[p].astype(BF16)
        tx[k] = jnp.dot(lhs, big, preferred_element_type=F32) + jnp.dot(lhs, small, preferred_element_type=F32)
        return carry

    lax.fori_loop(0, slots, mean_tile, 0, unroll=4)

    per = 1.0 / functools.reduce(jnp.add, [scales[k] * tx[k, 6:7, :] for k in range(slots)])
    for c in range(3):
        acc = jnp.zeros((8, C), F32)
        for k in range(slots):
            rows = tx[k, c:c + 1, :] + tx[k, 3 + c:4 + c, :] + tx[k, 19 + c:20 + c, :]
            acc = acc + scales[k] * rows
        xbar[8 * c:8 * c + 8, :] = acc * per
    W = C // Y_HI

    def lanes(who):
        return pl.ds(pl.multiple_of(who * W, W), W)

    xybuf[h] = xbar[:, lanes(h)]
    for at, peer in zip(y_at, y_peers):
        send(6, xbar.at[:, lanes(at)], xybuf.at[h], peer)

    both = over_y_done(1)
    over_z(1, both)

    set_bias(cl[0] + u)
    row8_one = jnp.where(row8 < 3, 1.0, 0.0)
    blank = jnp.zeros((8, C), F32)

    def plan_tile(k, carry):
        p = ts_ref[0, 0, k]
        one, two, three = split3(-tops[pl.ds(k, 1), :])
        shift = jnp.where(row8 == 0, one, jnp.where(row8 == 1, two, jnp.where(row8 == 2, three, 0.0)))
        pick = jnp.where(row24 == p, 1.0, 0.0)
        lhs = jnp.concatenate([ys[tt_ref[0, 0, k]], pick, shift, blank], 0).astype(BF16)
        rhs = jnp.concatenate([xs[p], bias[...], row8_one, blank], 0).astype(BF16)
        e = jnp.exp2(lax.dot_general(lhs, rhs, (((0,), (0,)), ((), ())), preferred_element_type=F32))
        big = e.astype(BF16)
        ehi[k] = big
        elo[k] = (e - big.astype(F32)).astype(BF16)
        return carry
    lax.fori_loop(0, slots, plan_tile, 0, unroll=4)
    f_all = (u + cl[3]) * BACK
    for c in range(CPD):
        f_out[:, c * C:(c + 1) * C] = f_all[c:c + 1, :]
    stores[0].start()
    done = waiter(6, xybuf.at[pl.ds(0, Y_HI - 1)])
    done.wait_recv()
    done.wait_send()

    def weighted(buf, weight_buf, n, total_block):
        acc = jnp.zeros((24, W), F32)
        for k in range(n):
            part = jnp.exp2(weight_buf[k, :, lanes(h)] - total_block)
            acc = acc + buf[k] * jnp.concatenate([part, part, part], 0)
        return acc

    xzbuf[z] = weighted(xybuf, ybuf.at[1], Y_HI, zbuf[1, z, :, lanes(h)])
    for peer in z_peers:
        send(7, xzbuf.at[z], xzbuf.at[z], peer)
    v = -over_z_done(1)

    cl[2] = v
    wlog = cl[1] + v
    bias[0:8, :] = wlog

    def grad_tile(k, carry):
        q = tt_ref[0, 0, k]
        w = jnp.exp2(bias[pl.ds(q, 1), :] + tops[pl.ds(k, 1), :])
        one, two, three = split3(yt[q] * w)
        lhs = jnp.concatenate([one, two, three], 0).astype(BF16)
        out = (jnp.dot(lhs, ehi[k], preferred_element_type=F32)
               + jnp.dot(lhs, elo[k], preferred_element_type=F32))
        gs[k] = out[0:8, :] + out[8:16, :] + out[16:24, :]
        return carry
    lax.fori_loop(0, slots, grad_tile, 0, unroll=4)

    if n_z > 1:
        done = waiter(7, xzbuf.at[pl.ds(0, n_z - 1)])
        done.wait_recv()
        done.wait_send()
    xtbuf[h] = weighted(xzbuf, zbuf.at[1], n_z, -cl[2, :, lanes(h)])
    for peer in y_peers:
        send(9, xtbuf.at[h], xtbuf.at[h], peer)

    own = owners(ts_ref)
    share = CPD * C // n_tgt
    per_cluster = C // share
    for c in range(CPD):
        acc = jnp.zeros((8, C), F32)
        for k in range(slots):
            acc = acc + jnp.where(own[k] == c, gs[k], 0.0)
        diff = (xt[c] * acc[6:7, :] - acc) * (1.0 / R)
        for part in range(per_cluster):
            dsend[c * per_cluster + part] = diff[0:4, part * share:(part + 1) * share]
    dbuf[t] = dsend[t]
    for at, peer in zip(tgt_at, tgt_peers):
        send(8, dsend.at[at], dbuf.at[t], peer)

    g_all = (cl[2] + cl[4]) * BACK
    for c in range(CPD):
        g_out[:, c * C:(c + 1) * C] = g_all[c:c + 1, :]
    stores[1].start()

    done = waiter(8, dbuf.at[pl.ds(0, n_tgt - 1)])
    done.wait_recv()
    done.wait_send()
    grad = functools.reduce(jnp.add, [dbuf[k] for k in range(n_tgt)])
    sg_out[...] = grad[0:3, :]
    stores[2].start()

    done = waiter(9, xtbuf.at[pl.ds(0, Y_HI - 1)])
    done.wait_recv()
    done.wait_send()
    for k in range(Y_HI):
        block = xtbuf[k] * (1.0 / R)
        for q in range(CPD):
            at = pl.ds(q * C + k * W, W)
            mean = jnp.concatenate([block[8 * c + q:8 * c + q + 1, :] for c in range(3)], 0)
            tg_out[:, at] = b_ref[:, at] * (y_ref[:, at] - mean)
    stores[3].start()
    for store in stores:
        store.wait()


def copy_kernel(*refs):
    n = (len(refs) - 1) // 3
    sem = refs[-1]
    loads = [pltpu.make_async_copy(refs[k], refs[2 * n + k], sem.at[k]) for k in range(n)]
    stores = [pltpu.make_async_copy(refs[2 * n + k], refs[n + k], sem.at[n + k]) for k in range(n)]
    for load in loads:
        load.start()
    for load, store in zip(loads, stores):
        load.wait()
        store.start()
    for store in stores:
        store.wait()


def hand_out(*arrays):
    n = len(arrays)
    return pl.pallas_call(
        copy_kernel,
        out_shape=tuple(jax.ShapeDtypeStruct(a.shape, a.dtype) for a in arrays),
        in_specs=[pl.BlockSpec(memory_space=pltpu.HBM)] * n,
        out_specs=(pl.BlockSpec(memory_space=pltpu.HBM),) * n,
        scratch_shapes=[pltpu.VMEM(a.shape, a.dtype) for a in arrays] + [pltpu.SemaphoreType.DMA((2 * n,))],
        compiler_params=pltpu.CompilerParams(vmem_limit_bytes=56 * 1024 * 1024),
        name="hand_out",
    )(*arrays)


def body(x, y, a, b, g, ts, tt, tc):
    n_src = lax.axis_size("src")
    n_tgt = lax.axis_size("tgt")
    slots = ts.shape[2]
    width = x.shape[1]
    C = width // CPD
    share = width // n_tgt
    n_z = n_src // Y_HI
    V = pltpu.VMEM
    f, g1, sg, tg = pl.pallas_call(
        functools.partial(kernel, n_src, n_tgt, slots, C),
        out_shape=(jax.ShapeDtypeStruct((1, width), F32), jax.ShapeDtypeStruct((1, width), F32),
                   jax.ShapeDtypeStruct((3, share), F32), jax.ShapeDtypeStruct((3, width), F32)),
        in_specs=[pl.BlockSpec(memory_space=pltpu.HBM)] * 8,
        out_specs=(pl.BlockSpec(memory_space=pltpu.HBM),) * 4,
        scratch_shapes=[
            V((3, width), F32), V((3, width), F32), V((1, width), F32), V((1, width), F32), V((1, width), F32),
            pltpu.SMEM((1, 1, slots), jnp.int32), pltpu.SMEM((1, 1, slots), jnp.int32),
            pltpu.SMEM((1, 1), jnp.int32),
            V((1, width), F32), V((1, width), F32), V((3, share), F32), V((3, width), F32),
            V((CPD, 24, C), F32), V((CPD, 24, C), F32), V((CPD, 8, C), F32), V((CPD, 8, C), F32),
            V((5, 8, C), F32), V((24, C), F32), V((16, C), F32), V((16, C), F32), V((C, C), F32), V((C, 128), F32), V((slots, C, C), F32),
            V((slots, C, C), F32), V((slots, C, C), BF16), V((slots, C, C), BF16), V((slots, 24, C), F32), V((slots, 8, C), F32),
            V((ITERS, n_tgt, 8, C), F32), V((ITERS, Y_HI, 8, C), F32), V((ITERS, n_z, 8, C), F32),
            V((24, C), F32), V((Y_HI, 24, C // Y_HI), F32), V((n_z, 24, C // Y_HI), F32),
            V((Y_HI, 24, C // Y_HI), F32), V((n_tgt, 4, share), F32), V((n_tgt, 4, share), F32),
            pltpu.SemaphoreType.DMA((8,)), pltpu.SemaphoreType.DMA((4,)), pltpu.SemaphoreType.DMA((10,)), pltpu.SemaphoreType.DMA((10,)),
        ],
        compiler_params=pltpu.CompilerParams(collective_id=0, has_side_effects=True,
                                             vmem_limit_bytes=56 * 1024 * 1024),
        name="sinkhorn",
    )(x, y, a.reshape(1, -1), b.reshape(1, -1), g.reshape(1, -1), ts, tt, tc)
    f, g1, sg, tg = hand_out(f, g1, sg, tg)
    return f.reshape(-1), g1.reshape(-1), sg, tg


def solution(mesh):
    return jax.shard_map(
        body,
        mesh=mesh,
        in_specs=(P(None, "src"), P(None, "tgt"), P("src"), P("tgt"), P("tgt"),
                  P("src", "tgt", None), P("src", "tgt", None), P("src", "tgt")),
        out_specs=(P("src"), P("tgt"), P(None, ("src", "tgt")), P(None, "tgt")),
        check_vma=False,
    )
```

```python
import functools
import math

import jax
import jax.numpy as jnp
from jax import lax
from jax.experimental import pallas as pl
from jax.experimental.pallas import tpu as pltpu
from jax.sharding import PartitionSpec as P

ITERS = 2
CPD = 8
Y_HI = 4
EPSILON = 0.02
FLOOR = -1e30
R = math.sqrt(math.log2(math.e) / EPSILON)
BACK = EPSILON * math.log(2.0)
MESH = pl.DeviceIdType.MESH
F32 = jnp.float32
BF16 = jnp.bfloat16


def split3(v):
    one = v.astype(BF16).astype(F32)
    rest = v - one
    two = rest.astype(BF16).astype(F32)
    return one, two, rest - two


def logsum(parts):
    top = functools.reduce(jnp.maximum, parts)
    return top + jnp.log2(functools.reduce(jnp.add, [jnp.exp2(p - top) for p in parts]))


def kernel(n_src, n_tgt, slots, C, *refs):
    ins, refs = refs[:8], refs[8:]
    outs, refs = refs[:4], refs[4:]
    held, refs = refs[:8], refs[8:]
    (f_out, g_out, sg_out, tg_out), refs = refs[:4], refs[4:]
    (xs, ys, xt, yt, cl, bias, tops, sums, held_scores, columns, row_scores, col_scores, ehi, elo, tx, gs,
     rbuf, ybuf, zbuf, xbar, xybuf, xzbuf, xtbuf, dsend, dbuf, insem, outsem, ssem, rsem) = refs
    x_ref, y_ref, a_ref, b_ref, g_ref, ts_ref, tt_ref, tc_ref = held
    fetches = [pltpu.make_async_copy(ins[k], held[k], insem.at[k]) for k in range(8)]
    for fetch in fetches:
        fetch.start()
    stores = [pltpu.make_async_copy((f_out, g_out, sg_out, tg_out)[k], outs[k], outsem.at[k]) for k in range(4)]
    n_z = n_src // Y_HI
    s = lax.axis_index("src")
    t = lax.axis_index("tgt")
    z = s // Y_HI
    h = lax.rem(s, Y_HI)
    n_lo = n_tgt // 8
    t_lo, t_x, t_core = t // 8, lax.rem(t // 2, 4), lax.rem(t, 2)
    steps = [(dy, dx, dc) for dy in range(n_lo) for dx in range(4) for dc in range(2)][1:]
    steps.sort(key=lambda d: -(d[0] + min(d[1], 4 - d[1]) + 0.1 * d[2]))
    tgt_at = [lax.rem(t_lo + dy, n_lo) * 8 + lax.rem(t_x + dx, 4) * 2 + lax.rem(t_core + dc, 2)
              for dy, dx, dc in steps]
    tgt_peers = [(s, at) for at in tgt_at]
    y_at = [lax.rem(h + k, Y_HI) for k in (2, 1, 3)]
    y_peers = [(z * Y_HI + at, t) for at in y_at]
    z_peers = [(lax.rem(z + k, n_z) * Y_HI + h, t)
               for k in sorted(range(1, n_z), key=lambda k: -min(k, n_z - k))]
    everyone = tgt_peers + y_peers + z_peers

    barrier = pltpu.get_barrier_semaphore()
    for peer in everyone:
        pl.semaphore_signal(barrier, inc=1, device_id=peer, device_id_type=MESH)

    def send(no, src, dst, peer):
        pltpu.make_async_remote_copy(src_ref=src, dst_ref=dst, send_sem=ssem.at[no], recv_sem=rsem.at[no],
                                     device_id=peer, device_id_type=MESH).start()

    def waiter(no, like):
        return pltpu.make_async_remote_copy(src_ref=like, dst_ref=like, send_sem=ssem.at[no], recv_sem=rsem.at[no],
                                            device_id=everyone[0], device_id_type=MESH)

    for k in (0, 1, 3, 4, 5, 6, 7):
        fetches[k].wait()
    row8 = lax.broadcasted_iota(jnp.int32, (8, C), 0)
    row24 = lax.rem(lax.broadcasted_iota(jnp.int32, (24, C), 0), 8)
    def half_norm(v):
        return 0.5 * jnp.sum(jnp.where(row8 < 3, v * v, 0.0), axis=0, keepdims=True)

    for c in range(CPD):
        at = pl.ds(c * C, C)
        for ref, full, stat, norm, ones in ((x_ref, xt, xs, 3, 1.0), (y_ref, yt, ys, 4, 0.0)):
            p3 = ref[:, at] * R
            full[c, 0:3, :] = p3
            full[c, 3:6, :] = p3
            full[c, 6:8, :] = jnp.ones((2, C), F32)
            v = full[c]
            coord = row8 < 6
            one, two, three = split3(jnp.where(coord, v, 0.0))
            if norm == 3:
                a = jnp.where(row8 < 3, one, two) + jnp.where(row8 == 6, 1.0, 0.0)
                stat[c] = jnp.concatenate([a, jnp.where(row8 < 3, one, two), jnp.where(row8 < 3, one, three)], 0)
            else:
                stat[c] = jnp.concatenate([one, two, jnp.where(row8 < 3, three, one)], 0)
                cl[norm, c:c + 1, :] = half_norm(v)
        cl[1, c:c + 1, :] = b_ref[:, at]
        cl[2, c:c + 1, :] = g_ref[:, at]
    cl[1] = jnp.log2(cl[1])
    v = cl[2] * (1.0 / BACK) - cl[4]

    count = tc_ref[0, 0]

    def owners(ref):
        return [jnp.where(k < count, ref[0, 0, k], -1) for k in range(slots)]

    def tile_scores(summed, own, summed_index, own_index):
        lhs = jnp.concatenate([summed[summed_index], bias[...]], 0).astype(BF16)
        pick = jnp.where(row24 == summed_index, 1.0, 0.0)
        rhs = jnp.concatenate([own[own_index], pick], 0).astype(BF16)
        return lax.dot_general(lhs, rhs, (((0,), (0,)), ((), ())), preferred_element_type=F32)

    def set_bias(value):
        one, two, three = split3(value)
        bias[0:8, :] = one
        bias[8:16, :] = two
        bias[16:24, :] = three

    def first_pass(value):
        set_bias(value)

        def scores_of(k):
            scores = tile_scores(ys, xs, tt_ref[0, 0, k], ts_ref[0, 0, k])
            held_scores[...] = scores
            return jnp.max(scores, axis=0, keepdims=True)

        def tile(k, top):
            acc = None
            for i in range(0, C, 16):
                part = held_scores[i:i + 16, :]
                row_scores[k, i:i + 16, :] = part
                e = jnp.exp2(part - top)
                acc = e if acc is None else acc + e
            tops[pl.ds(k, 1), :] = top
            sums[pl.ds(k, 1), :] = jnp.sum(acc, axis=0, keepdims=True)
            return scores_of(jnp.minimum(k + 1, slots - 1))
        lax.fori_loop(0, slots, tile, scores_of(0), unroll=4)

    def kept_pass(value, scores, summed_ref, keep=None):
        for c in range(CPD):
            columns[c] = jnp.broadcast_to(value[c:c + 1, :], (128, C)).T

        def exps_at(k, i, top, acc):
            e = jnp.exp2(held_scores[i:i + 8, :] - top)
            if keep is not None:
                keep[k, i:i + 8, :] = e
            return e if acc is None else acc + e

        def biased_at(k, c, i, most):
            column = columns[c, i:i + 8, :]
            v = scores[k, i:i + 8, :] + jnp.concatenate([column] * (C // 128), 1)
            held_scores[i:i + 8, :] = v
            return v if most is None else jnp.maximum(most, v)

        def put(k, top, acc):
            tops[pl.ds(k, 1), :] = top
            sums[pl.ds(k, 1), :] = jnp.sum(acc, axis=0, keepdims=True)

        def tile(k, top):
            c = summed_ref[0, 0, k + 1]
            acc = most = None
            for i in range(0, C, 8):
                acc = exps_at(k, i, top, acc)
                most = biased_at(k + 1, c, i, most)
            put(k, top, acc)
            return jnp.max(most, axis=0, keepdims=True)

        c = summed_ref[0, 0, 0]
        most = None
        for i in range(0, C, 8):
            most = biased_at(0, c, i, most)
        top = lax.fori_loop(0, slots - 1, tile, jnp.max(most, axis=0, keepdims=True))
        acc = None
        for i in range(0, C, 8):
            acc = exps_at(slots - 1, i, top, acc)
        put(slots - 1, top, acc)

    def merge(own_ref):
        own = owners(own_ref)
        masks = [row8 == own[k] for k in range(slots)]
        top = jnp.full((8, C), FLOOR, F32)
        for k in range(slots):
            top = jnp.maximum(top, jnp.where(masks[k], tops[k:k + 1, :], FLOOR))
        scales = [jnp.where(masks[k], jnp.exp2(tops[k:k + 1, :] - top), 0.0) for k in range(slots)]
        total = functools.reduce(jnp.add, [scales[k] * sums[k:k + 1, :] for k in range(slots)])
        return top + jnp.log2(total), scales, total

    def over_tgt(turn, local):
        buf = rbuf.at[turn]
        buf[t] = local
        for peer in tgt_peers:
            send(turn, buf.at[t], buf.at[t], peer)

    def over_tgt_done(turn):
        buf = rbuf.at[turn]
        done = waiter(turn, buf.at[pl.ds(0, n_tgt - 1)])
        done.wait_recv()
        done.wait_send()
        return -logsum([buf[k] for k in range(n_tgt)])

    def over_y(turn, local):
        buf = ybuf.at[turn]
        buf[h] = local
        for peer in y_peers:
            send(2 + turn, buf.at[h], buf.at[h], peer)

    def over_y_done(turn):
        buf = ybuf.at[turn]
        done = waiter(2 + turn, buf.at[pl.ds(0, Y_HI - 1)])
        done.wait_recv()
        done.wait_send()
        return logsum([buf[k] for k in range(Y_HI)])

    def over_z(turn, local):
        buf = zbuf.at[turn]
        buf[z] = local
        for peer in z_peers:
            send(4 + turn, buf.at[z], buf.at[z], peer)

    def over_z_done(turn):
        buf = zbuf.at[turn]
        if n_z > 1:
            done = waiter(4 + turn, buf.at[pl.ds(0, n_z - 1)])
            done.wait_recv()
            done.wait_send()
        return logsum([buf[k] for k in range(n_z)])

    first_pass(cl[1] + v)
    start = v
    local = merge(ts_ref)[0]
    pl.semaphore_wait(barrier, len(everyone))
    over_tgt(0, local)

    def score_tile(k, carry):
        col_scores[k] = lax.dot_general(xs[ts_ref[0, 0, k]].astype(BF16), ys[tt_ref[0, 0, k]].astype(BF16),
                                        (((0,), (0,)), ((), ())), preferred_element_type=F32)
        return carry
    lax.fori_loop(0, slots, score_tile, 0, unroll=4)
    fetches[2].wait()
    for c in range(CPD):
        cl[0, c:c + 1, :] = a_ref[:, c * C:(c + 1) * C]
        cl[3, c:c + 1, :] = half_norm(xt[c])
    cl[0] = jnp.log2(cl[0])
    u = over_tgt_done(0)
    kept_pass(cl[0] + u, col_scores, ts_ref)
    over_y(0, merge(tt_ref)[0])
    over_z(0, over_y_done(0))
    v = -over_z_done(0)

    kept_pass(v - start, row_scores, tt_ref)
    over_tgt(1, merge(ts_ref)[0])
    u = over_tgt_done(1)
    exps = row_scores
    kept_pass(cl[0] + u, col_scores, ts_ref, keep=exps)
    local, scales, _ = merge(tt_ref)
    over_y(1, local)

    def mean_tile(k, carry):
        p = ts_ref[0, 0, k]
        e = exps[k]
        big = e.astype(BF16)
        small = (e - big.astype(F32)).astype(BF16)
        lhs = jnp.concatenate([xs[p, 0:8, :], xs[p, 16:24, :]], 0).astype(BF16)
        tx[k] = jnp.dot(lhs, big, preferred_element_type=F32) + jnp.dot(lhs, small, preferred_element_type=F32)
        return carry

    lax.fori_loop(0, slots, mean_tile, 0, unroll=4)

    per = 1.0 / functools.reduce(jnp.add, [scales[k] * tx[k, 6:7, :] for k in range(slots)])
    for c in range(3):
        acc = jnp.zeros((8, C), F32)
        for k in range(slots):
            rows = tx[k, c:c + 1, :] + tx[k, 3 + c:4 + c, :] + tx[k, 11 + c:12 + c, :]
            acc = acc + scales[k] * rows
        xbar[8 * c:8 * c + 8, :] = acc * per
    W = C // Y_HI

    def lanes(who):
        return pl.ds(pl.multiple_of(who * W, W), W)

    xybuf[h] = xbar[:, lanes(h)]
    for at, peer in zip(y_at, y_peers):
        send(6, xbar.at[:, lanes(at)], xybuf.at[h], peer)

    both = over_y_done(1)
    over_z(1, both)

    set_bias(cl[0] + u)
    row8_one = jnp.where(row8 < 3, 1.0, 0.0)
    blank = jnp.zeros((8, C), F32)

    def plan_tile(k, carry):
        p = ts_ref[0, 0, k]
        one, two, three = split3(-tops[pl.ds(k, 1), :])
        shift = jnp.where(row8 == 0, one, jnp.where(row8 == 1, two, jnp.where(row8 == 2, three, 0.0)))
        pick = jnp.where(row24 == p, 1.0, 0.0)
        lhs = jnp.concatenate([ys[tt_ref[0, 0, k]], pick, shift, blank], 0).astype(BF16)
        rhs = jnp.concatenate([xs[p], bias[...], row8_one, blank], 0).astype(BF16)
        e = jnp.exp2(lax.dot_general(lhs, rhs, (((0,), (0,)), ((), ())), preferred_element_type=F32))
        big = e.astype(BF16)
        ehi[k] = big
        elo[k] = (e - big.astype(F32)).astype(BF16)
        return carry
    lax.fori_loop(0, slots, plan_tile, 0, unroll=4)
    f_all = (u + cl[3]) * BACK
    for c in range(CPD):
        f_out[:, c * C:(c + 1) * C] = f_all[c:c + 1, :]
    stores[0].start()
    done = waiter(6, xybuf.at[pl.ds(0, Y_HI - 1)])
    done.wait_recv()
    done.wait_send()

    def weighted(buf, weight_buf, n, total_block):
        acc = jnp.zeros((24, W), F32)
        for k in range(n):
            part = jnp.exp2(weight_buf[k, :, lanes(h)] - total_block)
            acc = acc + buf[k] * jnp.concatenate([part, part, part], 0)
        return acc

    xzbuf[z] = weighted(xybuf, ybuf.at[1], Y_HI, zbuf[1, z, :, lanes(h)])
    for peer in z_peers:
        send(7, xzbuf.at[z], xzbuf.at[z], peer)
    v = -over_z_done(1)

    cl[2] = v
    wlog = cl[1] + v
    bias[0:8, :] = wlog

    def grad_tile(k, carry):
        q = tt_ref[0, 0, k]
        w = jnp.exp2(bias[pl.ds(q, 1), :] + tops[pl.ds(k, 1), :])
        one, two, three = split3(yt[q] * w)
        lhs = jnp.concatenate([one, two + three], 0).astype(BF16)
        out = (jnp.dot(lhs, ehi[k], preferred_element_type=F32)
               + jnp.dot(lhs, elo[k], preferred_element_type=F32))
        gs[k] = out[0:8, :] + out[8:16, :]
        return carry
    lax.fori_loop(0, slots, grad_tile, 0, unroll=4)

    if n_z > 1:
        done = waiter(7, xzbuf.at[pl.ds(0, n_z - 1)])
        done.wait_recv()
        done.wait_send()
    xtbuf[h] = weighted(xzbuf, zbuf.at[1], n_z, -cl[2, :, lanes(h)])
    for peer in y_peers:
        send(9, xtbuf.at[h], xtbuf.at[h], peer)

    own = owners(ts_ref)
    share = CPD * C // n_tgt
    per_cluster = C // share
    for c in range(CPD):
        acc = jnp.zeros((8, C), F32)
        for k in range(slots):
            acc = acc + jnp.where(own[k] == c, gs[k], 0.0)
        diff = (xt[c] * acc[6:7, :] - acc) * (1.0 / R)
        for part in range(per_cluster):
            dsend[c * per_cluster + part] = diff[0:4, part * share:(part + 1) * share]
    dbuf[t] = dsend[t]
    for at, peer in zip(tgt_at, tgt_peers):
        send(8, dsend.at[at], dbuf.at[t], peer)

    g_all = (cl[2] + cl[4]) * BACK
    for c in range(CPD):
        g_out[:, c * C:(c + 1) * C] = g_all[c:c + 1, :]
    stores[1].start()

    done = waiter(8, dbuf.at[pl.ds(0, n_tgt - 1)])
    done.wait_recv()
    done.wait_send()
    grad = functools.reduce(jnp.add, [dbuf[k] for k in range(n_tgt)])
    sg_out[...] = grad[0:3, :]
    stores[2].start()

    done = waiter(9, xtbuf.at[pl.ds(0, Y_HI - 1)])
    done.wait_recv()
    done.wait_send()
    for k in range(Y_HI):
        block = xtbuf[k] * (1.0 / R)
        for q in range(CPD):
            at = pl.ds(q * C + k * W, W)
            mean = jnp.concatenate([block[8 * c + q:8 * c + q + 1, :] for c in range(3)], 0)
            tg_out[:, at] = b_ref[:, at] * (y_ref[:, at] - mean)
    stores[3].start()
    for store in stores:
        store.wait()


def copy_kernel(*refs):
    n = (len(refs) - 1) // 3
    sem = refs[-1]
    loads = [pltpu.make_async_copy(refs[k], refs[2 * n + k], sem.at[k]) for k in range(n)]
    stores = [pltpu.make_async_copy(refs[2 * n + k], refs[n + k], sem.at[n + k]) for k in range(n)]
    for load in loads:
        load.start()
    for load, store in zip(loads, stores):
        load.wait()
        store.start()
    for store in stores:
        store.wait()


def hand_out(*arrays):
    n = len(arrays)
    return pl.pallas_call(
        copy_kernel,
        out_shape=tuple(jax.ShapeDtypeStruct(a.shape, a.dtype) for a in arrays),
        in_specs=[pl.BlockSpec(memory_space=pltpu.HBM)] * n,
        out_specs=(pl.BlockSpec(memory_space=pltpu.HBM),) * n,
        scratch_shapes=[pltpu.VMEM(a.shape, a.dtype) for a in arrays] + [pltpu.SemaphoreType.DMA((2 * n,))],
        compiler_params=pltpu.CompilerParams(vmem_limit_bytes=56 * 1024 * 1024),
        name="hand_out",
    )(*arrays)


def body(x, y, a, b, g, ts, tt, tc):
    n_src = lax.axis_size("src")
    n_tgt = lax.axis_size("tgt")
    slots = ts.shape[2]
    width = x.shape[1]
    C = width // CPD
    share = width // n_tgt
    n_z = n_src // Y_HI
    V = pltpu.VMEM
    f, g1, sg, tg = pl.pallas_call(
        functools.partial(kernel, n_src, n_tgt, slots, C),
        out_shape=(jax.ShapeDtypeStruct((1, width), F32), jax.ShapeDtypeStruct((1, width), F32),
                   jax.ShapeDtypeStruct((3, share), F32), jax.ShapeDtypeStruct((3, width), F32)),
        in_specs=[pl.BlockSpec(memory_space=pltpu.HBM)] * 8,
        out_specs=(pl.BlockSpec(memory_space=pltpu.HBM),) * 4,
        scratch_shapes=[
            V((3, width), F32), V((3, width), F32), V((1, width), F32), V((1, width), F32), V((1, width), F32),
            pltpu.SMEM((1, 1, slots), jnp.int32), pltpu.SMEM((1, 1, slots), jnp.int32),
            pltpu.SMEM((1, 1), jnp.int32),
            V((1, width), F32), V((1, width), F32), V((3, share), F32), V((3, width), F32),
            V((CPD, 24, C), F32), V((CPD, 24, C), F32), V((CPD, 8, C), F32), V((CPD, 8, C), F32),
            V((5, 8, C), F32), V((24, C), F32), V((16, C), F32), V((16, C), F32), V((C, C), F32), V((CPD, C, 128), F32), V((slots, C, C), F32),
            V((slots, C, C), F32), V((slots, C, C), BF16), V((slots, C, C), BF16), V((slots, 16, C), F32), V((slots, 8, C), F32),
            V((ITERS, n_tgt, 8, C), F32), V((ITERS, Y_HI, 8, C), F32), V((ITERS, n_z, 8, C), F32),
            V((24, C), F32), V((Y_HI, 24, C // Y_HI), F32), V((n_z, 24, C // Y_HI), F32),
            V((Y_HI, 24, C // Y_HI), F32), V((n_tgt, 4, share), F32), V((n_tgt, 4, share), F32),
            pltpu.SemaphoreType.DMA((8,)), pltpu.SemaphoreType.DMA((4,)), pltpu.SemaphoreType.DMA((10,)), pltpu.SemaphoreType.DMA((10,)),
        ],
        compiler_params=pltpu.CompilerParams(collective_id=0, has_side_effects=True,
                                             vmem_limit_bytes=56 * 1024 * 1024),
        name="sinkhorn",
    )(x, y, a.reshape(1, -1), b.reshape(1, -1), g.reshape(1, -1), ts, tt, tc)
    f, g1, sg, tg = hand_out(f, g1, sg, tg)
    return f.reshape(-1), g1.reshape(-1), sg, tg


def solution(mesh):
    return jax.shard_map(
        body,
        mesh=mesh,
        in_specs=(P(None, "src"), P(None, "tgt"), P("src"), P("tgt"), P("tgt"),
                  P("src", "tgt", None), P("src", "tgt", None), P("src", "tgt")),
        out_specs=(P("src"), P("tgt"), P(None, ("src", "tgt")), P(None, "tgt")),
        check_vma=False,
    )
```

```python
import functools
import math

import jax
import jax.numpy as jnp
from jax import lax
from jax.experimental import pallas as pl
from jax.experimental.pallas import tpu as pltpu
from jax.sharding import PartitionSpec as P

ITERS = 2
CPD = 8
Y_HI = 4
EPSILON = 0.02
FLOOR = -1e30
R = math.sqrt(math.log2(math.e) / EPSILON)
BACK = EPSILON * math.log(2.0)
MESH = pl.DeviceIdType.MESH
F32 = jnp.float32
BF16 = jnp.bfloat16


def split3(v):
    one = v.astype(BF16).astype(F32)
    rest = v - one
    two = rest.astype(BF16).astype(F32)
    return one, two, rest - two


def logsum(parts):
    top = functools.reduce(jnp.maximum, parts)
    return top + jnp.log2(functools.reduce(jnp.add, [jnp.exp2(p - top) for p in parts]))


def kernel(n_src, n_tgt, slots, C, *refs):
    ins, refs = refs[:8], refs[8:]
    outs, refs = refs[:4], refs[4:]
    held, refs = refs[:8], refs[8:]
    (f_out, g_out, sg_out, tg_out), refs = refs[:4], refs[4:]
    (xs, ys, xt, yt, cl, bias, tops, sums, held_scores, columns, row_scores, col_scores, ehi, elo, tx, gs,
     rbuf, ybuf, zbuf, xbar, xybuf, xzbuf, xtbuf, dsend, dbuf, insem, outsem, ssem, rsem) = refs
    x_ref, y_ref, a_ref, b_ref, g_ref, ts_ref, tt_ref, tc_ref = held
    fetches = [pltpu.make_async_copy(ins[k], held[k], insem.at[k]) for k in range(8)]
    for fetch in fetches:
        fetch.start()
    stores = [pltpu.make_async_copy((f_out, g_out, sg_out, tg_out)[k], outs[k], outsem.at[k]) for k in range(4)]
    n_z = n_src // Y_HI
    s = lax.axis_index("src")
    t = lax.axis_index("tgt")
    z = s // Y_HI
    h = lax.rem(s, Y_HI)
    n_lo = n_tgt // 8
    t_lo, t_x, t_core = t // 8, lax.rem(t // 2, 4), lax.rem(t, 2)
    steps = [(dy, dx, dc) for dy in range(n_lo) for dx in range(4) for dc in range(2)][1:]
    steps.sort(key=lambda d: -(d[0] + min(d[1], 4 - d[1]) + 0.1 * d[2]))
    tgt_at = [lax.rem(t_lo + dy, n_lo) * 8 + lax.rem(t_x + dx, 4) * 2 + lax.rem(t_core + dc, 2)
              for dy, dx, dc in steps]
    tgt_peers = [(s, at) for at in tgt_at]
    y_at = [lax.rem(h + k, Y_HI) for k in (2, 1, 3)]
    y_peers = [(z * Y_HI + at, t) for at in y_at]
    z_peers = [(lax.rem(z + k, n_z) * Y_HI + h, t)
               for k in sorted(range(1, n_z), key=lambda k: -min(k, n_z - k))]
    everyone = tgt_peers + y_peers + z_peers

    barrier = pltpu.get_barrier_semaphore()
    for peer in everyone:
        pl.semaphore_signal(barrier, inc=1, device_id=peer, device_id_type=MESH)

    def send(no, src, dst, peer):
        pltpu.make_async_remote_copy(src_ref=src, dst_ref=dst, send_sem=ssem.at[no], recv_sem=rsem.at[no],
                                     device_id=peer, device_id_type=MESH).start()

    def waiter(no, like):
        return pltpu.make_async_remote_copy(src_ref=like, dst_ref=like, send_sem=ssem.at[no], recv_sem=rsem.at[no],
                                            device_id=everyone[0], device_id_type=MESH)

    for k in (0, 1, 3, 4, 5, 6, 7):
        fetches[k].wait()
    row8 = lax.broadcasted_iota(jnp.int32, (8, C), 0)
    row24 = lax.rem(lax.broadcasted_iota(jnp.int32, (24, C), 0), 8)
    def half_norm(v):
        return 0.5 * jnp.sum(jnp.where(row8 < 3, v * v, 0.0), axis=0, keepdims=True)

    for c in range(CPD):
        at = pl.ds(c * C, C)
        for ref, full, stat, norm, ones in ((x_ref, xt, xs, 3, 1.0), (y_ref, yt, ys, 4, 0.0)):
            p3 = ref[:, at] * R
            full[c, 0:3, :] = p3
            full[c, 3:6, :] = p3
            full[c, 6:8, :] = jnp.ones((2, C), F32)
            v = full[c]
            coord = row8 < 6
            one, two, three = split3(jnp.where(coord, v, 0.0))
            if norm == 3:
                a = jnp.where(row8 < 3, one, two) + jnp.where(row8 == 6, 1.0, 0.0)
                stat[c] = jnp.concatenate([a, jnp.where(row8 < 3, one, two), jnp.where(row8 < 3, one, three)], 0)
            else:
                stat[c] = jnp.concatenate([one, two, jnp.where(row8 < 3, three, one)], 0)
                cl[norm, c:c + 1, :] = half_norm(v)
        cl[1, c:c + 1, :] = b_ref[:, at]
        cl[2, c:c + 1, :] = g_ref[:, at]
    cl[1] = jnp.log2(cl[1])
    v = cl[2] * (1.0 / BACK) - cl[4]

    count = tc_ref[0, 0]

    def owners(ref):
        return [jnp.where(k < count, ref[0, 0, k], -1) for k in range(slots)]

    def tile_scores(summed, own, summed_index, own_index):
        lhs = jnp.concatenate([summed[summed_index], bias[...]], 0).astype(BF16)
        pick = jnp.where(row24 == summed_index, 1.0, 0.0)
        rhs = jnp.concatenate([own[own_index], pick], 0).astype(BF16)
        return lax.dot_general(lhs, rhs, (((0,), (0,)), ((), ())), preferred_element_type=F32)

    def set_bias(value):
        one, two, three = split3(value)
        bias[0:8, :] = one
        bias[8:16, :] = two
        bias[16:24, :] = three

    def first_pass(value):
        set_bias(value)

        def scores_of(k):
            scores = tile_scores(ys, xs, tt_ref[0, 0, k], ts_ref[0, 0, k])
            held_scores[...] = scores
            return jnp.max(scores, axis=0, keepdims=True)

        def tile(k, top):
            acc = None
            for i in range(0, C, 16):
                part = held_scores[i:i + 16, :]
                row_scores[k, i:i + 16, :] = part
                e = jnp.exp2(part - top)
                acc = e if acc is None else acc + e
            tops[pl.ds(k, 1), :] = top
            sums[pl.ds(k, 1), :] = jnp.sum(acc, axis=0, keepdims=True)
            return scores_of(jnp.minimum(k + 1, slots - 1))
        lax.fori_loop(0, slots, tile, scores_of(0), unroll=4)

    def kept_pass(value, scores, summed_ref, keep=None):
        bias[0:8, :] = value

        def turn(k):
            row = bias[pl.ds(summed_ref[0, 0, k], 1), :]
            columns[...] = jnp.broadcast_to(row, (128, C)).T

        def exps_at(k, i, top, acc):
            e = jnp.exp2(held_scores[i:i + 8, :] - top)
            if keep is not None:
                keep[k, i:i + 8, :] = e
            return e if acc is None else acc + e

        def biased_at(k, i, most):
            column = columns[i:i + 8, :]
            v = scores[k, i:i + 8, :] + jnp.concatenate([column] * (C // 128), 1)
            held_scores[i:i + 8, :] = v
            return v if most is None else jnp.maximum(most, v)

        def put(k, top, acc):
            tops[pl.ds(k, 1), :] = top
            sums[pl.ds(k, 1), :] = jnp.sum(acc, axis=0, keepdims=True)

        def tile(k, top):
            acc = most = None
            for i in range(0, C, 8):
                acc = exps_at(k, i, top, acc)
                most = biased_at(k + 1, i, most)
            turn(jnp.minimum(k + 2, slots - 1))
            put(k, top, acc)
            return jnp.max(most, axis=0, keepdims=True)

        turn(0)
        most = None
        for i in range(0, C, 8):
            most = biased_at(0, i, most)
        turn(1)
        top = lax.fori_loop(0, slots - 1, tile, jnp.max(most, axis=0, keepdims=True))
        acc = None
        for i in range(0, C, 8):
            acc = exps_at(slots - 1, i, top, acc)
        put(slots - 1, top, acc)

    def merge(own_ref):
        own = owners(own_ref)
        masks = [row8 == own[k] for k in range(slots)]
        top = jnp.full((8, C), FLOOR, F32)
        for k in range(slots):
            top = jnp.maximum(top, jnp.where(masks[k], tops[k:k + 1, :], FLOOR))
        scales = [jnp.where(masks[k], jnp.exp2(tops[k:k + 1, :] - top), 0.0) for k in range(slots)]
        total = functools.reduce(jnp.add, [scales[k] * sums[k:k + 1, :] for k in range(slots)])
        return top + jnp.log2(total), scales, total

    def over_tgt(turn, local):
        buf = rbuf.at[turn]
        buf[t] = local
        for peer in tgt_peers:
            send(turn, buf.at[t], buf.at[t], peer)

    def over_tgt_done(turn):
        buf = rbuf.at[turn]
        done = waiter(turn, buf.at[pl.ds(0, n_tgt - 1)])
        done.wait_recv()
        done.wait_send()
        return -logsum([buf[k] for k in range(n_tgt)])

    def over_y(turn, local):
        buf = ybuf.at[turn]
        buf[h] = local
        for peer in y_peers:
            send(2 + turn, buf.at[h], buf.at[h], peer)

    def over_y_done(turn):
        buf = ybuf.at[turn]
        done = waiter(2 + turn, buf.at[pl.ds(0, Y_HI - 1)])
        done.wait_recv()
        done.wait_send()
        return logsum([buf[k] for k in range(Y_HI)])

    def over_z(turn, local):
        buf = zbuf.at[turn]
        buf[z] = local
        for peer in z_peers:
            send(4 + turn, buf.at[z], buf.at[z], peer)

    def over_z_done(turn):
        buf = zbuf.at[turn]
        if n_z > 1:
            done = waiter(4 + turn, buf.at[pl.ds(0, n_z - 1)])
            done.wait_recv()
            done.wait_send()
        return logsum([buf[k] for k in range(n_z)])

    first_pass(cl[1] + v)
    start = v
    local = merge(ts_ref)[0]
    pl.semaphore_wait(barrier, len(everyone))
    over_tgt(0, local)

    def score_tile(k, carry):
        col_scores[k] = lax.dot_general(xs[ts_ref[0, 0, k]].astype(BF16), ys[tt_ref[0, 0, k]].astype(BF16),
                                        (((0,), (0,)), ((), ())), preferred_element_type=F32)
        return carry
    lax.fori_loop(0, slots, score_tile, 0, unroll=4)
    fetches[2].wait()
    for c in range(CPD):
        cl[0, c:c + 1, :] = a_ref[:, c * C:(c + 1) * C]
        cl[3, c:c + 1, :] = half_norm(xt[c])
    cl[0] = jnp.log2(cl[0])
    u = over_tgt_done(0)
    kept_pass(cl[0] + u, col_scores, ts_ref)
    over_y(0, merge(tt_ref)[0])
    over_z(0, over_y_done(0))
    v = -over_z_done(0)

    kept_pass(v - start, row_scores, tt_ref)
    over_tgt(1, merge(ts_ref)[0])
    u = over_tgt_done(1)
    exps = row_scores
    kept_pass(cl[0] + u, col_scores, ts_ref, keep=exps)
    local, scales, _ = merge(tt_ref)
    over_y(1, local)

    def mean_tile(k, carry):
        p = ts_ref[0, 0, k]
        e = exps[k]
        big = e.astype(BF16)
        small = (e - big.astype(F32)).astype(BF16)
        lhs = jnp.concatenate([xs[p, 0:8, :], xs[p, 16:24, :]], 0).astype(BF16)
        tx[k] = jnp.dot(lhs, big, preferred_element_type=F32) + jnp.dot(lhs, small, preferred_element_type=F32)
        return carry

    lax.fori_loop(0, slots, mean_tile, 0, unroll=4)

    per = 1.0 / functools.reduce(jnp.add, [scales[k] * tx[k, 6:7, :] for k in range(slots)])
    for c in range(3):
        acc = jnp.zeros((8, C), F32)
        for k in range(slots):
            rows = tx[k, c:c + 1, :] + tx[k, 3 + c:4 + c, :] + tx[k, 11 + c:12 + c, :]
            acc = acc + scales[k] * rows
        xbar[8 * c:8 * c + 8, :] = acc * per
    W = C // Y_HI

    def lanes(who):
        return pl.ds(pl.multiple_of(who * W, W), W)

    xybuf[h] = xbar[:, lanes(h)]
    for at, peer in zip(y_at, y_peers):
        send(6, xbar.at[:, lanes(at)], xybuf.at[h], peer)

    both = over_y_done(1)
    over_z(1, both)

    set_bias(cl[0] + u)
    row8_one = jnp.where(row8 < 3, 1.0, 0.0)
    blank = jnp.zeros((8, C), F32)

    def plan_tile(k, carry):
        p = ts_ref[0, 0, k]
        one, two, three = split3(-tops[pl.ds(k, 1), :])
        shift = jnp.where(row8 == 0, one, jnp.where(row8 == 1, two, jnp.where(row8 == 2, three, 0.0)))
        pick = jnp.where(row24 == p, 1.0, 0.0)
        lhs = jnp.concatenate([ys[tt_ref[0, 0, k]], pick, shift, blank], 0).astype(BF16)
        rhs = jnp.concatenate([xs[p], bias[...], row8_one, blank], 0).astype(BF16)
        e = jnp.exp2(lax.dot_general(lhs, rhs, (((0,), (0,)), ((), ())), preferred_element_type=F32))
        big = e.astype(BF16)
        ehi[k] = big
        elo[k] = (e - big.astype(F32)).astype(BF16)
        return carry
    lax.fori_loop(0, slots, plan_tile, 0, unroll=4)
    f_all = (u + cl[3]) * BACK
    for c in range(CPD):
        f_out[:, c * C:(c + 1) * C] = f_all[c:c + 1, :]
    stores[0].start()
    done = waiter(6, xybuf.at[pl.ds(0, Y_HI - 1)])
    done.wait_recv()
    done.wait_send()

    def weighted(buf, weight_buf, n, total_block):
        acc = jnp.zeros((24, W), F32)
        for k in range(n):
            part = jnp.exp2(weight_buf[k, :, lanes(h)] - total_block)
            acc = acc + buf[k] * jnp.concatenate([part, part, part], 0)
        return acc

    xzbuf[z] = weighted(xybuf, ybuf.at[1], Y_HI, zbuf[1, z, :, lanes(h)])
    for peer in z_peers:
        send(7, xzbuf.at[z], xzbuf.at[z], peer)
    v = -over_z_done(1)

    cl[2] = v
    wlog = cl[1] + v
    bias[0:8, :] = wlog

    def grad_tile(k, carry):
        q = tt_ref[0, 0, k]
        w = jnp.exp2(bias[pl.ds(q, 1), :] + tops[pl.ds(k, 1), :])
        one, two, three = split3(yt[q] * w)
        lhs = jnp.concatenate([one, two + three], 0).astype(BF16)
        out = (jnp.dot(lhs, ehi[k], preferred_element_type=F32)
               + jnp.dot(lhs, elo[k], preferred_element_type=F32))
        gs[k] = out[0:8, :] + out[8:16, :]
        return carry
    lax.fori_loop(0, slots, grad_tile, 0, unroll=4)

    if n_z > 1:
        done = waiter(7, xzbuf.at[pl.ds(0, n_z - 1)])
        done.wait_recv()
        done.wait_send()
    xtbuf[h] = weighted(xzbuf, zbuf.at[1], n_z, -cl[2, :, lanes(h)])
    for peer in y_peers:
        send(9, xtbuf.at[h], xtbuf.at[h], peer)

    own = owners(ts_ref)
    share = CPD * C // n_tgt
    per_cluster = C // share
    for c in range(CPD):
        acc = jnp.zeros((8, C), F32)
        for k in range(slots):
            acc = acc + jnp.where(own[k] == c, gs[k], 0.0)
        diff = (xt[c] * acc[6:7, :] - acc) * (1.0 / R)
        for part in range(per_cluster):
            dsend[c * per_cluster + part] = diff[0:4, part * share:(part + 1) * share]
    dbuf[t] = dsend[t]
    for at, peer in zip(tgt_at, tgt_peers):
        send(8, dsend.at[at], dbuf.at[t], peer)

    g_all = (cl[2] + cl[4]) * BACK
    for c in range(CPD):
        g_out[:, c * C:(c + 1) * C] = g_all[c:c + 1, :]
    stores[1].start()

    done = waiter(8, dbuf.at[pl.ds(0, n_tgt - 1)])
    done.wait_recv()
    done.wait_send()
    grad = functools.reduce(jnp.add, [dbuf[k] for k in range(n_tgt)])
    sg_out[...] = grad[0:3, :]
    stores[2].start()

    done = waiter(9, xtbuf.at[pl.ds(0, Y_HI - 1)])
    done.wait_recv()
    done.wait_send()
    for k in range(Y_HI):
        block = xtbuf[k] * (1.0 / R)
        for q in range(CPD):
            at = pl.ds(q * C + k * W, W)
            mean = jnp.concatenate([block[8 * c + q:8 * c + q + 1, :] for c in range(3)], 0)
            tg_out[:, at] = b_ref[:, at] * (y_ref[:, at] - mean)
    stores[3].start()
    for store in stores:
        store.wait()


def copy_kernel(*refs):
    n = (len(refs) - 1) // 3
    sem = refs[-1]
    loads = [pltpu.make_async_copy(refs[k], refs[2 * n + k], sem.at[k]) for k in range(n)]
    stores = [pltpu.make_async_copy(refs[2 * n + k], refs[n + k], sem.at[n + k]) for k in range(n)]
    for load in loads:
        load.start()
    for load, store in zip(loads, stores):
        load.wait()
        store.start()
    for store in stores:
        store.wait()


def hand_out(*arrays):
    n = len(arrays)
    return pl.pallas_call(
        copy_kernel,
        out_shape=tuple(jax.ShapeDtypeStruct(a.shape, a.dtype) for a in arrays),
        in_specs=[pl.BlockSpec(memory_space=pltpu.HBM)] * n,
        out_specs=(pl.BlockSpec(memory_space=pltpu.HBM),) * n,
        scratch_shapes=[pltpu.VMEM(a.shape, a.dtype) for a in arrays] + [pltpu.SemaphoreType.DMA((2 * n,))],
        compiler_params=pltpu.CompilerParams(vmem_limit_bytes=56 * 1024 * 1024),
        name="hand_out",
    )(*arrays)


def body(x, y, a, b, g, ts, tt, tc):
    n_src = lax.axis_size("src")
    n_tgt = lax.axis_size("tgt")
    slots = ts.shape[2]
    width = x.shape[1]
    C = width // CPD
    share = width // n_tgt
    n_z = n_src // Y_HI
    V = pltpu.VMEM
    f, g1, sg, tg = pl.pallas_call(
        functools.partial(kernel, n_src, n_tgt, slots, C),
        out_shape=(jax.ShapeDtypeStruct((1, width), F32), jax.ShapeDtypeStruct((1, width), F32),
                   jax.ShapeDtypeStruct((3, share), F32), jax.ShapeDtypeStruct((3, width), F32)),
        in_specs=[pl.BlockSpec(memory_space=pltpu.HBM)] * 8,
        out_specs=(pl.BlockSpec(memory_space=pltpu.HBM),) * 4,
        scratch_shapes=[
            V((3, width), F32), V((3, width), F32), V((1, width), F32), V((1, width), F32), V((1, width), F32),
            pltpu.SMEM((1, 1, slots), jnp.int32), pltpu.SMEM((1, 1, slots), jnp.int32),
            pltpu.SMEM((1, 1), jnp.int32),
            V((1, width), F32), V((1, width), F32), V((3, share), F32), V((3, width), F32),
            V((CPD, 24, C), F32), V((CPD, 24, C), F32), V((CPD, 8, C), F32), V((CPD, 8, C), F32),
            V((5, 8, C), F32), V((24, C), F32), V((16, C), F32), V((16, C), F32), V((C, C), F32), V((C, 128), F32), V((slots, C, C), F32),
            V((slots, C, C), F32), V((slots, C, C), BF16), V((slots, C, C), BF16), V((slots, 16, C), F32), V((slots, 8, C), F32),
            V((ITERS, n_tgt, 8, C), F32), V((ITERS, Y_HI, 8, C), F32), V((ITERS, n_z, 8, C), F32),
            V((24, C), F32), V((Y_HI, 24, C // Y_HI), F32), V((n_z, 24, C // Y_HI), F32),
            V((Y_HI, 24, C // Y_HI), F32), V((n_tgt, 4, share), F32), V((n_tgt, 4, share), F32),
            pltpu.SemaphoreType.DMA((8,)), pltpu.SemaphoreType.DMA((4,)), pltpu.SemaphoreType.DMA((10,)), pltpu.SemaphoreType.DMA((10,)),
        ],
        compiler_params=pltpu.CompilerParams(collective_id=0, has_side_effects=True,
                                             vmem_limit_bytes=56 * 1024 * 1024),
        name="sinkhorn",
    )(x, y, a.reshape(1, -1), b.reshape(1, -1), g.reshape(1, -1), ts, tt, tc)
    f, g1, sg, tg = hand_out(f, g1, sg, tg)
    return f.reshape(-1), g1.reshape(-1), sg, tg


def solution(mesh):
    return jax.shard_map(
        body,
        mesh=mesh,
        in_specs=(P(None, "src"), P(None, "tgt"), P("src"), P("tgt"), P("tgt"),
                  P("src", "tgt", None), P("src", "tgt", None), P("src", "tgt")),
        out_specs=(P("src"), P("tgt"), P(None, ("src", "tgt")), P(None, "tgt")),
        check_vma=False,
    )
```

```python
import functools
import math

import jax
import jax.numpy as jnp
from jax import lax
from jax.experimental import pallas as pl
from jax.experimental.pallas import tpu as pltpu
from jax.sharding import PartitionSpec as P

ITERS = 2
CPD = 8
Y_HI = 4
EPSILON = 0.02
FLOOR = -1e30
R = math.sqrt(math.log2(math.e) / EPSILON)
BACK = EPSILON * math.log(2.0)
MESH = pl.DeviceIdType.MESH
F32 = jnp.float32
BF16 = jnp.bfloat16


def split3(v):
    one = v.astype(BF16).astype(F32)
    rest = v - one
    two = rest.astype(BF16).astype(F32)
    return one, two, rest - two


def logsum(parts):
    top = functools.reduce(jnp.maximum, parts)
    return top + jnp.log2(functools.reduce(jnp.add, [jnp.exp2(p - top) for p in parts]))


def kernel(n_src, n_tgt, slots, C, *refs):
    ins, refs = refs[:8], refs[8:]
    outs, refs = refs[:4], refs[4:]
    held, refs = refs[:8], refs[8:]
    (f_out, g_out, sg_out, tg_out), refs = refs[:4], refs[4:]
    (xs, ys, xt, yt, cl, bias, tops, sums, held_scores, columns, row_scores, col_scores, ehi, elo, tx, gs,
     rbuf, ybuf, zbuf, xbar, xybuf, xzbuf, xtbuf, dsend, dbuf, insem, outsem, ssem, rsem) = refs
    x_ref, y_ref, a_ref, b_ref, g_ref, ts_ref, tt_ref, tc_ref = held
    fetches = [pltpu.make_async_copy(ins[k], held[k], insem.at[k]) for k in range(8)]
    for fetch in fetches:
        fetch.start()
    stores = [pltpu.make_async_copy((f_out, g_out, sg_out, tg_out)[k], outs[k], outsem.at[k]) for k in range(4)]
    n_z = n_src // Y_HI
    s = lax.axis_index("src")
    t = lax.axis_index("tgt")
    z = s // Y_HI
    h = lax.rem(s, Y_HI)
    n_lo = n_tgt // 8
    t_lo, t_x, t_core = t // 8, lax.rem(t // 2, 4), lax.rem(t, 2)
    steps = [(dy, dx, dc) for dy in range(n_lo) for dx in range(4) for dc in range(2)][1:]
    steps.sort(key=lambda d: -(d[0] + min(d[1], 4 - d[1]) + 0.1 * d[2]))
    tgt_at = [lax.rem(t_lo + dy, n_lo) * 8 + lax.rem(t_x + dx, 4) * 2 + lax.rem(t_core + dc, 2)
              for dy, dx, dc in steps]
    tgt_peers = [(s, at) for at in tgt_at]
    y_at = [lax.rem(h + k, Y_HI) for k in (2, 1, 3)]
    y_peers = [(z * Y_HI + at, t) for at in y_at]
    z_peers = [(lax.rem(z + k, n_z) * Y_HI + h, t)
               for k in sorted(range(1, n_z), key=lambda k: -min(k, n_z - k))]
    everyone = tgt_peers + y_peers + z_peers

    barrier = pltpu.get_barrier_semaphore()
    for peer in everyone:
        pl.semaphore_signal(barrier, inc=1, device_id=peer, device_id_type=MESH)

    def send(no, src, dst, peer):
        pltpu.make_async_remote_copy(src_ref=src, dst_ref=dst, send_sem=ssem.at[no], recv_sem=rsem.at[no],
                                     device_id=peer, device_id_type=MESH).start()

    def waiter(no, like):
        return pltpu.make_async_remote_copy(src_ref=like, dst_ref=like, send_sem=ssem.at[no], recv_sem=rsem.at[no],
                                            device_id=everyone[0], device_id_type=MESH)

    for k in (0, 1, 3, 4, 5, 6, 7):
        fetches[k].wait()
    row8 = lax.broadcasted_iota(jnp.int32, (8, C), 0)
    row24 = lax.rem(lax.broadcasted_iota(jnp.int32, (24, C), 0), 8)
    def half_norm(v):
        return 0.5 * jnp.sum(jnp.where(row8 < 3, v * v, 0.0), axis=0, keepdims=True)

    for c in range(CPD):
        at = pl.ds(c * C, C)
        for ref, full, stat, norm, ones in ((x_ref, xt, xs, 3, 1.0), (y_ref, yt, ys, 4, 0.0)):
            p3 = ref[:, at] * R
            full[c, 0:3, :] = p3
            full[c, 3:6, :] = p3
            full[c, 6:8, :] = jnp.ones((2, C), F32)
            v = full[c]
            coord = row8 < 6
            one, two, three = split3(jnp.where(coord, v, 0.0))
            if norm == 3:
                a = jnp.where(row8 < 3, one, two) + jnp.where(row8 == 6, 1.0, 0.0)
                stat[c] = jnp.concatenate([a, jnp.where(row8 < 3, one, two), jnp.where(row8 < 3, one, three)], 0)
            else:
                stat[c] = jnp.concatenate([one, two, jnp.where(row8 < 3, three, one)], 0)
                cl[norm, c:c + 1, :] = half_norm(v)
        cl[1, c:c + 1, :] = b_ref[:, at]
        cl[2, c:c + 1, :] = g_ref[:, at]
    cl[1] = jnp.log2(cl[1])
    v = cl[2] * (1.0 / BACK) - cl[4]

    count = tc_ref[0, 0]

    def owners(ref):
        return [jnp.where(k < count, ref[0, 0, k], -1) for k in range(slots)]

    def tile_scores(summed, own, summed_index, own_index):
        lhs = jnp.concatenate([summed[summed_index], bias[...]], 0).astype(BF16)
        pick = jnp.where(row24 == summed_index, 1.0, 0.0)
        rhs = jnp.concatenate([own[own_index], pick], 0).astype(BF16)
        return lax.dot_general(lhs, rhs, (((0,), (0,)), ((), ())), preferred_element_type=F32)

    def set_bias(value):
        one, two, three = split3(value)
        bias[0:8, :] = one
        bias[8:16, :] = two
        bias[16:24, :] = three

    def first_pass(value):
        set_bias(value)

        def scores_of(k):
            scores = tile_scores(ys, xs, tt_ref[0, 0, k], ts_ref[0, 0, k])
            held_scores[...] = scores
            return jnp.max(scores, axis=0, keepdims=True)

        def tile(k, top):
            acc = None
            for i in range(0, C, 16):
                part = held_scores[i:i + 16, :]
                row_scores[k, i:i + 16, :] = part
                e = jnp.exp2(part - top)
                acc = e if acc is None else acc + e
            tops[pl.ds(k, 1), :] = top
            sums[pl.ds(k, 1), :] = jnp.sum(acc, axis=0, keepdims=True)
            return scores_of(jnp.minimum(k + 1, slots - 1))
        lax.fori_loop(0, slots, tile, scores_of(0), unroll=4)

    def kept_pass(value, scores, summed_ref, keep=None):
        bias[0:8, :] = value

        def turn(k):
            row = bias[pl.ds(summed_ref[0, 0, k], 1), :]
            columns[...] = jnp.broadcast_to(row, (128, C)).T

        def exps_at(k, i, top, acc):
            e = jnp.exp2(held_scores[i:i + 8, :] - top)
            if keep is not None:
                keep[k, i:i + 8, :] = e
            return e if acc is None else acc + e

        def biased_at(k, i, most):
            column = columns[i:i + 8, :]
            v = scores[k, i:i + 8, :] + jnp.concatenate([column] * (C // 128), 1)
            held_scores[i:i + 8, :] = v
            return v if most is None else jnp.maximum(most, v)

        def put(k, top, acc):
            tops[pl.ds(k, 1), :] = top
            sums[pl.ds(k, 1), :] = jnp.sum(acc, axis=0, keepdims=True)

        def tile(k, top):
            acc = most = None
            for i in range(0, C, 8):
                acc = exps_at(k, i, top, acc)
                most = biased_at(k + 1, i, most)
            turn(jnp.minimum(k + 2, slots - 1))
            put(k, top, acc)
            return jnp.max(most, axis=0, keepdims=True)

        turn(0)
        most = None
        for i in range(0, C, 8):
            most = biased_at(0, i, most)
        turn(1)
        top = lax.fori_loop(0, slots - 1, tile, jnp.max(most, axis=0, keepdims=True))
        acc = None
        for i in range(0, C, 8):
            acc = exps_at(slots - 1, i, top, acc)
        put(slots - 1, top, acc)

    def merge(own_ref):
        own = owners(own_ref)
        masks = [row8 == own[k] for k in range(slots)]
        top = jnp.full((8, C), FLOOR, F32)
        for k in range(slots):
            top = jnp.maximum(top, jnp.where(masks[k], tops[k:k + 1, :], FLOOR))
        scales = [jnp.where(masks[k], jnp.exp2(tops[k:k + 1, :] - top), 0.0) for k in range(slots)]
        total = functools.reduce(jnp.add, [scales[k] * sums[k:k + 1, :] for k in range(slots)])
        return top + jnp.log2(total), scales, total

    def over_tgt(turn, local):
        buf = rbuf.at[turn]
        buf[t] = local
        for peer in tgt_peers:
            send(turn, buf.at[t], buf.at[t], peer)

    def over_tgt_done(turn):
        buf = rbuf.at[turn]
        done = waiter(turn, buf.at[pl.ds(0, n_tgt - 1)])
        done.wait_recv()
        done.wait_send()
        return -logsum([buf[k] for k in range(n_tgt)])

    def over_y(turn, local):
        buf = ybuf.at[turn]
        buf[h] = local
        for peer in y_peers:
            send(2 + turn, buf.at[h], buf.at[h], peer)

    def over_y_done(turn):
        buf = ybuf.at[turn]
        done = waiter(2 + turn, buf.at[pl.ds(0, Y_HI - 1)])
        done.wait_recv()
        done.wait_send()
        return logsum([buf[k] for k in range(Y_HI)])

    def over_z(turn, local):
        buf = zbuf.at[turn]
        buf[z] = local
        for peer in z_peers:
            send(4 + turn, buf.at[z], buf.at[z], peer)

    def over_z_done(turn):
        buf = zbuf.at[turn]
        if n_z > 1:
            done = waiter(4 + turn, buf.at[pl.ds(0, n_z - 1)])
            done.wait_recv()
            done.wait_send()
        return logsum([buf[k] for k in range(n_z)])

    first_pass(cl[1] + v)
    start = v
    local = merge(ts_ref)[0]
    pl.semaphore_wait(barrier, len(everyone))
    over_tgt(0, local)

    def score_tile(k, carry):
        col_scores[k] = lax.dot_general(xs[ts_ref[0, 0, k]].astype(BF16), ys[tt_ref[0, 0, k]].astype(BF16),
                                        (((0,), (0,)), ((), ())), preferred_element_type=F32)
        return carry
    lax.fori_loop(0, slots, score_tile, 0, unroll=4)
    fetches[2].wait()
    for c in range(CPD):
        cl[0, c:c + 1, :] = a_ref[:, c * C:(c + 1) * C]
        cl[3, c:c + 1, :] = half_norm(xt[c])
    cl[0] = jnp.log2(cl[0])
    u = over_tgt_done(0)
    kept_pass(cl[0] + u, col_scores, ts_ref)
    over_z(0, merge(tt_ref)[0])
    over_y(0, over_z_done(0))
    v = -over_y_done(0)

    kept_pass(v - start, row_scores, tt_ref)
    over_tgt(1, merge(ts_ref)[0])
    u = over_tgt_done(1)
    exps = row_scores
    kept_pass(cl[0] + u, col_scores, ts_ref, keep=exps)
    local, scales, _ = merge(tt_ref)
    over_y(1, local)

    def mean_tile(k, carry):
        p = ts_ref[0, 0, k]
        e = exps[k]
        big = e.astype(BF16)
        small = (e - big.astype(F32)).astype(BF16)
        lhs = jnp.concatenate([xs[p, 0:8, :], xs[p, 16:24, :]], 0).astype(BF16)
        tx[k] = jnp.dot(lhs, big, preferred_element_type=F32) + jnp.dot(lhs, small, preferred_element_type=F32)
        return carry

    lax.fori_loop(0, slots, mean_tile, 0, unroll=4)

    per = 1.0 / functools.reduce(jnp.add, [scales[k] * tx[k, 6:7, :] for k in range(slots)])
    for c in range(3):
        acc = jnp.zeros((8, C), F32)
        for k in range(slots):
            rows = tx[k, c:c + 1, :] + tx[k, 3 + c:4 + c, :] + tx[k, 11 + c:12 + c, :]
            acc = acc + scales[k] * rows
        xbar[8 * c:8 * c + 8, :] = acc * per
    W = C // Y_HI

    def lanes(who):
        return pl.ds(pl.multiple_of(who * W, W), W)

    xybuf[h] = xbar[:, lanes(h)]
    for at, peer in zip(y_at, y_peers):
        send(6, xbar.at[:, lanes(at)], xybuf.at[h], peer)

    both = over_y_done(1)
    over_z(1, both)

    set_bias(cl[0] + u)
    row8_one = jnp.where(row8 < 3, 1.0, 0.0)
    blank = jnp.zeros((8, C), F32)

    def plan_tile(k, carry):
        p = ts_ref[0, 0, k]
        one, two, three = split3(-tops[pl.ds(k, 1), :])
        shift = jnp.where(row8 == 0, one, jnp.where(row8 == 1, two, jnp.where(row8 == 2, three, 0.0)))
        pick = jnp.where(row24 == p, 1.0, 0.0)
        lhs = jnp.concatenate([ys[tt_ref[0, 0, k]], pick, shift, blank], 0).astype(BF16)
        rhs = jnp.concatenate([xs[p], bias[...], row8_one, blank], 0).astype(BF16)
        e = jnp.exp2(lax.dot_general(lhs, rhs, (((0,), (0,)), ((), ())), preferred_element_type=F32))
        big = e.astype(BF16)
        ehi[k] = big
        elo[k] = (e - big.astype(F32)).astype(BF16)
        return carry
    lax.fori_loop(0, slots, plan_tile, 0, unroll=4)
    f_all = (u + cl[3]) * BACK
    for c in range(CPD):
        f_out[:, c * C:(c + 1) * C] = f_all[c:c + 1, :]
    stores[0].start()
    done = waiter(6, xybuf.at[pl.ds(0, Y_HI - 1)])
    done.wait_recv()
    done.wait_send()

    def weighted(buf, weight_buf, n, total_block):
        acc = jnp.zeros((24, W), F32)
        for k in range(n):
            part = jnp.exp2(weight_buf[k, :, lanes(h)] - total_block)
            acc = acc + buf[k] * jnp.concatenate([part, part, part], 0)
        return acc

    xzbuf[z] = weighted(xybuf, ybuf.at[1], Y_HI, zbuf[1, z, :, lanes(h)])
    for peer in z_peers:
        send(7, xzbuf.at[z], xzbuf.at[z], peer)
    v = -over_z_done(1)

    cl[2] = v
    wlog = cl[1] + v
    bias[0:8, :] = wlog

    def grad_tile(k, carry):
        q = tt_ref[0, 0, k]
        w = jnp.exp2(bias[pl.ds(q, 1), :] + tops[pl.ds(k, 1), :])
        one, two, three = split3(yt[q] * w)
        lhs = jnp.concatenate([one, two + three], 0).astype(BF16)
        out = (jnp.dot(lhs, ehi[k], preferred_element_type=F32)
               + jnp.dot(lhs, elo[k], preferred_element_type=F32))
        gs[k] = out[0:8, :] + out[8:16, :]
        return carry
    lax.fori_loop(0, slots, grad_tile, 0, unroll=4)

    if n_z > 1:
        done = waiter(7, xzbuf.at[pl.ds(0, n_z - 1)])
        done.wait_recv()
        done.wait_send()
    xtbuf[h] = weighted(xzbuf, zbuf.at[1], n_z, -cl[2, :, lanes(h)])
    for peer in y_peers:
        send(9, xtbuf.at[h], xtbuf.at[h], peer)

    own = owners(ts_ref)
    share = CPD * C // n_tgt
    per_cluster = C // share
    for c in range(CPD):
        acc = jnp.zeros((8, C), F32)
        for k in range(slots):
            acc = acc + jnp.where(own[k] == c, gs[k], 0.0)
        diff = (xt[c] * acc[6:7, :] - acc) * (1.0 / R)
        for part in range(per_cluster):
            dsend[c * per_cluster + part] = diff[0:4, part * share:(part + 1) * share]
    dbuf[t] = dsend[t]
    for at, peer in zip(tgt_at, tgt_peers):
        send(8, dsend.at[at], dbuf.at[t], peer)

    g_all = (cl[2] + cl[4]) * BACK
    for c in range(CPD):
        g_out[:, c * C:(c + 1) * C] = g_all[c:c + 1, :]
    stores[1].start()

    done = waiter(8, dbuf.at[pl.ds(0, n_tgt - 1)])
    done.wait_recv()
    done.wait_send()
    grad = functools.reduce(jnp.add, [dbuf[k] for k in range(n_tgt)])
    sg_out[...] = grad[0:3, :]
    stores[2].start()

    done = waiter(9, xtbuf.at[pl.ds(0, Y_HI - 1)])
    done.wait_recv()
    done.wait_send()
    for k in range(Y_HI):
        block = xtbuf[k] * (1.0 / R)
        for q in range(CPD):
            at = pl.ds(q * C + k * W, W)
            mean = jnp.concatenate([block[8 * c + q:8 * c + q + 1, :] for c in range(3)], 0)
            tg_out[:, at] = b_ref[:, at] * (y_ref[:, at] - mean)
    stores[3].start()
    for store in stores:
        store.wait()


def copy_kernel(*refs):
    n = (len(refs) - 1) // 3
    sem = refs[-1]
    loads = [pltpu.make_async_copy(refs[k], refs[2 * n + k], sem.at[k]) for k in range(n)]
    stores = [pltpu.make_async_copy(refs[2 * n + k], refs[n + k], sem.at[n + k]) for k in range(n)]
    for load in loads:
        load.start()
    for load, store in zip(loads, stores):
        load.wait()
        store.start()
    for store in stores:
        store.wait()


def hand_out(*arrays):
    n = len(arrays)
    return pl.pallas_call(
        copy_kernel,
        out_shape=tuple(jax.ShapeDtypeStruct(a.shape, a.dtype) for a in arrays),
        in_specs=[pl.BlockSpec(memory_space=pltpu.HBM)] * n,
        out_specs=(pl.BlockSpec(memory_space=pltpu.HBM),) * n,
        scratch_shapes=[pltpu.VMEM(a.shape, a.dtype) for a in arrays] + [pltpu.SemaphoreType.DMA((2 * n,))],
        compiler_params=pltpu.CompilerParams(vmem_limit_bytes=56 * 1024 * 1024),
        name="hand_out",
    )(*arrays)


def body(x, y, a, b, g, ts, tt, tc):
    n_src = lax.axis_size("src")
    n_tgt = lax.axis_size("tgt")
    slots = ts.shape[2]
    width = x.shape[1]
    C = width // CPD
    share = width // n_tgt
    n_z = n_src // Y_HI
    V = pltpu.VMEM
    f, g1, sg, tg = pl.pallas_call(
        functools.partial(kernel, n_src, n_tgt, slots, C),
        out_shape=(jax.ShapeDtypeStruct((1, width), F32), jax.ShapeDtypeStruct((1, width), F32),
                   jax.ShapeDtypeStruct((3, share), F32), jax.ShapeDtypeStruct((3, width), F32)),
        in_specs=[pl.BlockSpec(memory_space=pltpu.HBM)] * 8,
        out_specs=(pl.BlockSpec(memory_space=pltpu.HBM),) * 4,
        scratch_shapes=[
            V((3, width), F32), V((3, width), F32), V((1, width), F32), V((1, width), F32), V((1, width), F32),
            pltpu.SMEM((1, 1, slots), jnp.int32), pltpu.SMEM((1, 1, slots), jnp.int32),
            pltpu.SMEM((1, 1), jnp.int32),
            V((1, width), F32), V((1, width), F32), V((3, share), F32), V((3, width), F32),
            V((CPD, 24, C), F32), V((CPD, 24, C), F32), V((CPD, 8, C), F32), V((CPD, 8, C), F32),
            V((5, 8, C), F32), V((24, C), F32), V((16, C), F32), V((16, C), F32), V((C, C), F32), V((C, 128), F32), V((slots, C, C), F32),
            V((slots, C, C), F32), V((slots, C, C), BF16), V((slots, C, C), BF16), V((slots, 16, C), F32), V((slots, 8, C), F32),
            V((ITERS, n_tgt, 8, C), F32), V((ITERS, Y_HI, 8, C), F32), V((ITERS, n_z, 8, C), F32),
            V((24, C), F32), V((Y_HI, 24, C // Y_HI), F32), V((n_z, 24, C // Y_HI), F32),
            V((Y_HI, 24, C // Y_HI), F32), V((n_tgt, 4, share), F32), V((n_tgt, 4, share), F32),
            pltpu.SemaphoreType.DMA((8,)), pltpu.SemaphoreType.DMA((4,)), pltpu.SemaphoreType.DMA((10,)), pltpu.SemaphoreType.DMA((10,)),
        ],
        compiler_params=pltpu.CompilerParams(collective_id=0, has_side_effects=True,
                                             vmem_limit_bytes=56 * 1024 * 1024),
        name="sinkhorn",
    )(x, y, a.reshape(1, -1), b.reshape(1, -1), g.reshape(1, -1), ts, tt, tc)
    f, g1, sg, tg = hand_out(f, g1, sg, tg)
    return f.reshape(-1), g1.reshape(-1), sg, tg


def solution(mesh):
    return jax.shard_map(
        body,
        mesh=mesh,
        in_specs=(P(None, "src"), P(None, "tgt"), P("src"), P("tgt"), P("tgt"),
                  P("src", "tgt", None), P("src", "tgt", None), P("src", "tgt")),
        out_specs=(P("src"), P("tgt"), P(None, ("src", "tgt")), P(None, "tgt")),
        check_vma=False,
    )
```
